32 devices in a mesh: grp: 4 (over x, core), dom: 8 (over z, y).
Axes of the slice: x: 2, y: 2, z: 4, core: 2. Of those that a mesh axis runs over, the one named last changes fastest.
Arguments:
- nodes: bfloat16 [32768, 256], P(('grp', 'dom')), may hold values from -8 to 8
- neighbours: int32 [32768, 8], P(('grp', 'dom')), may hold values from 0 to 1279
- send_rows: int32 [8192], P(('grp', 'dom')), may hold values from 0 to 1023
- landmark_ids: int32 [8192], P(('grp', 'dom')), may hold values from 0 to 1023
- w_dst: bfloat16 [256, 256], replicated, may hold values from -0.375 to 0.375
- w_src: bfloat16 [256, 256], replicated, may hold values from -0.375 to 0.375
- w_msg: bfloat16 [256, 256], replicated, may hold values from -0.375 to 0.375
- edge_bias: float32 [256], replicated, may hold values from -4 to 4
- w_query: bfloat16 [256, 256], replicated, may hold values from -0.375 to 0.375
- w_key: bfloat16 [256, 256], replicated, may hold values from -0.375 to 0.375
- w_value: bfloat16 [256, 256], replicated, may hold values from -0.375 to 0.375
- w_out: bfloat16 [256, 256], replicated, may hold values from -0.375 to 0.375
Outputs:
- result: bfloat16 [32768, 256], P(('grp', 'dom'))
- kernel_term: float32 [32768, 256], P(('grp', 'dom'))
The draws below stay inside these ranges and needn't reach their ends.
Inputs may be any that keep to these rules, and one draw needn't show every extreme that they name: `neighbours`: entries index the device's own 1024 rows, then the 128 rows received from the previous partition, then the 128 rows from the next one. `send_rows`: each partition's entries are rows of its own nodes. `landmark_ids`: each partition's entries are rows of its own nodes.
All inputs are finite; a program needn't handle non-finite values.
Results may differ from the reference program's by a relative error of at most 0.0054.
Values may be sent and summed in bfloat16 or wider, within the bound.
No kernel may reach another device: no remote copies, remote signals or barrier semaphores. Data moves between devices by JAX's collectives and lax.ppermute only.
A program may use at most 64 MiB of HBM per device.

```python
import math
import jax
import jax.numpy as jnp
from jax import lax

C = 256
M = 8192
NBR = 8
ROWS = 1024
HALO = 128
NODES = 32768
DEVICES = 32


def draw_nodes(key, part):
    base = jax.random.fold_in(key, 17)
    noise_key, direction_key = jax.random.split(base, 2)
    partitions = NODES // ROWS
    noise = jax.random.normal(noise_key, (partitions, ROWS, C), jnp.float32)
    amplitude = 2.0
    direction = jax.random.normal(direction_key, (partitions, 1, C), jnp.float32)
    values = jnp.clip(noise + amplitude * direction, -8.0, 8.0)
    return values.reshape(NODES, C).astype(jnp.bfloat16)


def touch_ends(values, own_key, smallest, largest):
    spot = [jax.random.randint(jax.random.fold_in(own_key, axis), (), 0, length) for axis, length in enumerate(values.shape)]
    main_axis = values.shape.index(max(values.shape))
    neighbour = spot[:main_axis] + [(spot[main_axis] + 1) % values.shape[main_axis]] + spot[main_axis + 1:]
    return values.at[tuple(spot)].set(smallest).at[tuple(neighbour)].set(largest)


def centred(stream_key, dims, deviation, limit, dtype=jnp.bfloat16):
    return jnp.clip(deviation * jax.random.normal(stream_key, dims, jnp.float32), -limit, limit).astype(dtype)


def setup_inputs(seed: int = 0) -> dict:
    streams_of = jax.random.split(jax.random.key(seed), 13)
    return {
        "nodes": draw_nodes(jax.random.fold_in(streams_of[12], 71), 0),
        "neighbours": touch_ends(jax.random.randint(streams_of[1], (NODES, NBR), 0, ROWS + 2 * HALO), jax.random.fold_in(streams_of[1], 1), 0, (ROWS + 2 * HALO) - 1).astype(jnp.int32),
        "send_rows": touch_ends(jax.random.randint(streams_of[2], (2 * HALO * DEVICES,), 0, ROWS), jax.random.fold_in(streams_of[2], 1), 0, ROWS - 1).astype(jnp.int32),
        "landmark_ids": touch_ends(jax.random.randint(streams_of[3], (M,), 0, ROWS), jax.random.fold_in(streams_of[3], 1), 0, ROWS - 1).astype(jnp.int32),
        "w_dst": centred(streams_of[4], (C, C), C ** -0.5, 0.375),
        "w_src": centred(streams_of[5], (C, C), C ** -0.5, 0.375),
        "w_msg": centred(streams_of[6], (C, C), C ** -0.5, 0.375),
        "edge_bias": centred(streams_of[7], (C,), 1.0, 4.0, jnp.float32),
        "w_query": centred(streams_of[8], (C, C), C ** -0.5, 0.375),
        "w_key": centred(streams_of[9], (C, C), C ** -0.5, 0.375),
        "w_value": centred(streams_of[10], (C, C), C ** -0.5, 0.375),
        "w_out": centred(streams_of[11], (C, C), C ** -0.5, 0.375),
    }


def rms_scale(values):
    return values * lax.rsqrt(lax.optimization_barrier(jnp.mean(values * values, axis=-1, keepdims=True)) + 1e-06)

def reference(nodes, neighbours, send_rows, landmark_ids, w_dst, w_src, w_msg, edge_bias, w_query, w_key, w_value, w_out):
    parts = nodes.reshape(DEVICES, ROWS, C)
    sends = send_rows.reshape(DEVICES, 2 * HALO)
    outgoing = jax.vmap(lambda block, picks: block[picks])(parts, sends)
    from_prev = jnp.roll(outgoing[:, HALO:], 1, axis=0)
    from_next = jnp.roll(outgoing[:, :HALO], -1, axis=0)
    extended = jnp.concatenate([parts, from_prev, from_next], axis=1)
    links = neighbours.reshape(DEVICES, ROWS, NBR)

    def edge_layer(inputs):
        block, table, slots = inputs
        source = jnp.dot(table, w_src, preferred_element_type=jnp.float32)
        target = jnp.dot(block, w_dst, preferred_element_type=jnp.float32)
        preact = target[:, None, :] + source[slots] + edge_bias
        messages = lax.optimization_barrier(jnp.mean(jax.nn.gelu(preact), axis=1)).astype(jnp.bfloat16)
        return (block.astype(jnp.float32) + jnp.dot(messages, w_msg, preferred_element_type=jnp.float32)).astype(jnp.bfloat16)
    updated = lax.map(edge_layer, (parts, extended, links))
    normed = rms_scale(updated.astype(jnp.float32)).astype(jnp.bfloat16)
    flat = normed.reshape(NODES, C)
    query = jnp.dot(flat, w_query, preferred_element_type=jnp.float32).astype(jnp.bfloat16)
    value = jnp.dot(flat, w_value, preferred_element_type=jnp.float32).astype(jnp.bfloat16)
    chosen = jax.vmap(lambda block, picks: block[picks])(normed, landmark_ids.reshape(DEVICES, M // DEVICES)).reshape(M, C)
    keys = jnp.dot(chosen, w_key, preferred_element_type=jnp.float32).astype(jnp.bfloat16)
    scale = 2.0 * C ** (-0.5)
    block_size = math.gcd(M, 256)

    def landmark_block(key_rows):
        kernel = jnp.exp(jnp.dot(query, key_rows.T, preferred_element_type=jnp.float32) * scale).astype(jnp.bfloat16)
        return lax.dot_general(kernel, value, (((0,), (0,)), ((), ())), preferred_element_type=jnp.float32)
    sums = lax.map(landmark_block, keys.reshape(M // block_size, block_size, C)).reshape(M, C)
    landmark_sums = sums.astype(jnp.bfloat16)

    def node_block(query_rows):
        kernel = jnp.exp(jnp.dot(query_rows, keys.T, preferred_element_type=jnp.float32) * scale).astype(jnp.bfloat16)
        smooth = jnp.dot(kernel, landmark_sums, preferred_element_type=jnp.float32)
        return rms_scale(smooth)
    kernel_term = lax.map(node_block, query.reshape(DEVICES, ROWS, C)).reshape(NODES, C)
    scaled = kernel_term.astype(jnp.bfloat16)
    result = updated.reshape(NODES, C).astype(jnp.float32) + jnp.dot(scaled, w_out, preferred_element_type=jnp.float32)
    return (result.astype(jnp.bfloat16), kernel_term)
```

```python
import functools
import math

import jax
import jax.numpy as jnp
from jax import lax
from jax.experimental import pallas as pl
from jax.experimental.pallas import tpu as pltpu
from jax.sharding import PartitionSpec as P

BF16 = jnp.bfloat16
F32 = jnp.float32
BOTH = ("grp", "dom")
EPS = 1e-06
VMEM_LIMIT = 48 * 2**20


def dot(a, b, ca=1, cb=0):
    return lax.dot_general(a, b, (((ca,), (cb,)), ((), ())), preferred_element_type=F32)


def whole(shape):
    return pl.BlockSpec(shape, lambda *_: (0,) * len(shape))


def call(body, name, out_shape, in_specs, out_specs, args, grid=(1,), scratch=(), flops=0, exps=0):
    outs = out_shape if isinstance(out_shape, (list, tuple)) else [out_shape]
    moved = sum(a.size * a.dtype.itemsize for a in (*args, *outs))
    return pl.pallas_call(
        body,
        grid=grid,
        in_specs=in_specs,
        out_specs=out_specs,
        out_shape=out_shape,
        scratch_shapes=list(scratch),
        name=name,
        compiler_params=pltpu.CompilerParams(vmem_limit_bytes=VMEM_LIMIT),
        cost_estimate=pl.CostEstimate(flops=flops, bytes_accessed=moved, transcendentals=exps),
    )(*args)


def picked(ids, table):
    rows = table.shape[0]
    place = lax.broadcasted_iota(jnp.int32, (rows, ids.shape[1]), 0)
    hot = jnp.where(place == ids, 1.0, 0.0).astype(BF16)
    return dot(hot, table, 0, 0).astype(BF16)


def send_body(ids_ref, nodes_ref, prev_ref, next_ref):
    rows = picked(ids_ref[...], nodes_ref[...])
    half = rows.shape[0] // 2
    prev_ref[...] = rows[:half]
    next_ref[...] = rows[half:]


def hot_rows(ids, first, width):
    n = ids.shape[1]
    spread = jnp.transpose(jnp.broadcast_to(ids, (128, n)))
    lane = lax.broadcasted_iota(jnp.int32, (n, 128), 1)
    parts = [
        jnp.where(spread == lane + (first + 128 * c), 1.0, 0.0).astype(BF16)
        for c in range(width // 128)
    ]
    return jnp.concatenate(parts, axis=1)


def own_body(links_ref, nodes_ref, tile_ref, w_src_ref, w_dst_ref, bias_ref, pre_ref, source):
    @pl.when(pl.program_id(0) == 0)
    def _():
        source[...] = dot(nodes_ref[...], w_src_ref[...]).astype(BF16)

    target = dot(tile_ref[...], w_dst_ref[...]) + bias_ref[...]
    links = links_ref[...]
    for k in range(links.shape[0]):
        hot = hot_rows(links[k : k + 1], 0, source.shape[0])
        pre_ref[k] = dot(hot, source[...]) + target


def gelu(x):
    inner = math.sqrt(2.0 / math.pi) * (x + 0.044715 * (x * x * x))
    return 0.5 * x * (1.0 + jnp.tanh(inner))


def edge_body(
    links_ref,
    pre_ref,
    prev_ref,
    next_ref,
    tile_ref,
    ids_ref,
    w_src_ref,
    w_msg_ref,
    w_key_ref,
    updated_ref,
    normed_ref,
    keys_ref,
    source,
    table,
):
    step = pl.program_id(0)
    halo = prev_ref.shape[0]
    rows = table.shape[0]

    @pl.when(step == 0)
    def _():
        source[:halo] = dot(prev_ref[...], w_src_ref[...]).astype(BF16)
        source[halo:] = dot(next_ref[...], w_src_ref[...]).astype(BF16)

    links = links_ref[...]
    count = links.shape[0]
    total = 0.0
    for k in range(count):
        hot = hot_rows(links[k : k + 1], rows, 2 * halo)
        total += gelu(pre_ref[k] + dot(hot, source[...]))
    messages = (total * (1.0 / count)).astype(BF16)
    updated = (tile_ref[...].astype(F32) + dot(messages, w_msg_ref[...])).astype(BF16)
    updated_ref[...] = updated
    wide = updated.astype(F32)
    normed = (wide * lax.rsqrt(jnp.mean(wide * wide, axis=1, keepdims=True) + EPS)).astype(BF16)
    normed_ref[...] = normed
    n = normed.shape[0]
    table[pl.ds(pl.multiple_of(step * n, n), n), :] = normed

    @pl.when(step == pl.num_programs(0) - 1)
    def _():
        keys_ref[...] = dot(picked(ids_ref[...], table[...]), w_key_ref[...]).astype(BF16)


def smooth_up_body(count, scale, has_start, *refs):
    nodes, refs = refs[:count], refs[count:]
    keys_ref, w_query_ref, w_value_ref, *refs = refs
    if has_start:
        start_ref, *refs = refs
    tiles, refs = refs[:count], refs[count:]
    sums_ref, *refs = refs
    query, value = refs[:count], refs[count:]

    @pl.when(pl.program_id(0) == 0)
    def _():
        for b in range(count):
            query[b][...] = dot(nodes[b][...], w_query_ref[...]).astype(BF16)
            value[b][...] = dot(nodes[b][...], w_value_ref[...]).astype(BF16)

    total = start_ref[...] if has_start else 0.0
    for b in range(count):
        tile = jnp.exp2(dot(keys_ref[...], query[b][...], 1, 1) * scale).astype(BF16)
        tiles[b][...] = tile
        total += dot(tile, value[b][...])
    sums_ref[...] = total.astype(sums_ref.dtype)


def smooth_up(blocks, keys, w_query, w_value, start, out_dtype, name):
    marks, c = keys.shape
    step = min(marks, 512)
    scale = 2.0 * c ** (-0.5) * math.log2(math.e)
    sizes = [b.shape[0] for b in blocks]
    in_specs = [whole(b.shape) for b in blocks]
    in_specs += [pl.BlockSpec((step, c), lambda j: (j, 0)), whole((c, c)), whole((c, c))]
    args = [*blocks, keys, w_query, w_value]
    if start is not None:
        in_specs.append(pl.BlockSpec((step, c), lambda j: (j, 0)))
        args.append(start)
    out = call(
        functools.partial(smooth_up_body, len(blocks), scale, start is not None),
        name,
        [jax.ShapeDtypeStruct((marks, n), BF16) for n in sizes]
        + [jax.ShapeDtypeStruct((marks, c), out_dtype)],
        in_specs,
        [pl.BlockSpec((step, n), lambda j: (j, 0)) for n in sizes]
        + [pl.BlockSpec((step, c), lambda j: (j, 0))],
        args,
        grid=(marks // step,),
        scratch=[pltpu.VMEM((n, c), BF16) for n in sizes] * 2,
        flops=4 * marks * sum(sizes) * c + 4 * sum(sizes) * c * c,
        exps=marks * sum(sizes),
    )
    return out[:-1], out[-1]


def smooth_down_body(tile_ref, sums_ref, out_ref):
    out_ref[...] = dot(tile_ref[...], sums_ref[...], 0, 0).astype(out_ref.dtype)


def smooth_down(tiles, sums, out_dtype, name):
    marks, n = tiles.shape
    c = sums.shape[1]
    step = min(n, 256)
    return call(
        smooth_down_body,
        name,
        jax.ShapeDtypeStruct((n, c), out_dtype),
        [pl.BlockSpec((marks, step), lambda j: (0, j)), whole((marks, c))],
        pl.BlockSpec((step, c), lambda j: (j, 0)),
        [tiles, sums],
        grid=(n // step,),
        flops=2 * marks * n * c,
    )


def last_body(own_ref, a_ref, b_ref, c_ref, updated_ref, w_out_ref, result_ref, term_ref):
    smooth = own_ref[...] + a_ref[...].astype(F32) + b_ref[...].astype(F32) + c_ref[...].astype(F32)
    term = smooth * lax.rsqrt(jnp.mean(smooth * smooth, axis=1, keepdims=True) + EPS)
    term_ref[...] = term
    result = updated_ref[...].astype(F32) + dot(term.astype(BF16), w_out_ref[...])
    result_ref[...] = result.astype(BF16)


def shards(
    groups,
    domains,
    nodes,
    neighbours,
    send_rows,
    landmark_ids,
    w_dst,
    w_src,
    w_msg,
    edge_bias,
    w_query,
    w_key,
    w_value,
    w_out,
):
    rows, c = nodes.shape
    halo = send_rows.shape[0] // 2
    mine = landmark_ids.shape[0]
    slots = neighbours.shape[1]
    line = domains // 2
    parts = groups * domains
    half = rows // 2

    def pair(axis, size, flip):
        return lambda v: lax.ppermute(v, axis, [(i, i ^ flip) for i in range(size)])

    over_core = pair("grp", groups, 1)
    over_x = pair("grp", groups, 2)
    over_y = pair("dom", domains, 1)
    over_z = [pair("dom", domains, 2 * t) for t in range(line)]
    over_xy = lambda v: lax.ppermute(
        v,
        BOTH,
        [
            (g * domains + d, (g ^ 2) * domains + (d ^ 1))
            for g in range(groups)
            for d in range(domains)
        ],
    )

    to_prev, to_next = call(
        send_body,
        "send_rows",
        [jax.ShapeDtypeStruct((halo, c), BF16)] * 2,
        [whole((1, 2 * halo)), whole((rows, c))],
        [whole((halo, c))] * 2,
        [send_rows.reshape(1, 2 * halo), nodes],
        flops=4 * halo * rows * c,
    )
    from_prev = lax.ppermute(to_next, BOTH, [(i, (i + 1) % parts) for i in range(parts)])
    from_next = lax.ppermute(to_prev, BOTH, [((i + 1) % parts, i) for i in range(parts)])

    links = neighbours.T
    tile = min(rows, 256)
    steps = rows // tile
    links_spec = pl.BlockSpec((slots, tile), lambda i: (0, i))
    tile_spec = pl.BlockSpec((tile, c), lambda i: (i, 0))
    pre_spec = pl.BlockSpec((slots, tile, c), lambda i: (0, i, 0))
    pre = call(
        own_body,
        "own_edges",
        jax.ShapeDtypeStruct((slots, rows, c), F32),
        [links_spec, whole((rows, c)), tile_spec, whole((c, c)), whole((c, c)), whole((1, c))],
        pre_spec,
        [links, nodes, nodes, w_src, w_dst, edge_bias.reshape(1, c)],
        grid=(steps,),
        scratch=[pltpu.VMEM((rows, c), BF16)],
        flops=2 * slots * rows * rows * c,
    )
    updated, normed, keys = call(
        edge_body,
        "edges",
        [
            jax.ShapeDtypeStruct((rows, c), BF16),
            jax.ShapeDtypeStruct((rows, c), BF16),
            jax.ShapeDtypeStruct((mine, c), BF16),
        ],
        [
            links_spec,
            pre_spec,
            whole((halo, c)),
            whole((halo, c)),
            tile_spec,
            whole((1, mine)),
            whole((c, c)),
            whole((c, c)),
            whole((c, c)),
        ],
        [tile_spec, tile_spec, whole((mine, c))],
        [
            links,
            pre,
            from_prev,
            from_next,
            nodes,
            landmark_ids.reshape(1, mine),
            w_src,
            w_msg,
            w_key,
        ],
        grid=(steps,),
        scratch=[pltpu.VMEM((2 * halo, c), BF16), pltpu.VMEM((rows, c), BF16)],
        flops=4 * slots * rows * halo * c,
        exps=slots * rows * c,
    )

    side_keys = jnp.concatenate([keys] + [over_z[t](keys) for t in range(1, line)], axis=0)
    normed_x = over_x(normed)
    normed_y = over_y(normed)
    all_keys = jnp.concatenate([side_keys, over_core(side_keys)], axis=0)
    normed_a = over_y(normed_x[:half])
    normed_b = over_x(normed_y[half:])

    (own_tiles,), sums = smooth_up([normed], all_keys, w_query, w_value, None, F32, "up_own")
    (x_tiles, y_tiles), sums = smooth_up(
        [normed_x, normed_y], all_keys, w_query, w_value, sums, F32, "up_xy"
    )
    (a_tiles, b_tiles), sums = smooth_up(
        [normed_a, normed_b], all_keys, w_query, w_value, sums, BF16, "up_diagonal"
    )

    side = line * mine
    side_sums = (sums[:side].astype(F32) + over_core(sums[side:]).astype(F32)).astype(BF16)
    blocks = [side_sums[t * mine : (t + 1) * mine] for t in range(line)]
    arrived = [over_z[t](blocks[t]) for t in range(1, line)]
    total = blocks[0].astype(F32)
    for block in arrived:
        total = total + block.astype(F32)
    total = total.astype(BF16)
    side_total = jnp.concatenate([total] + [over_z[t](total) for t in range(1, line)], axis=0)
    all_total = jnp.concatenate([side_total, over_core(side_total)], axis=0)

    a_part = smooth_down(a_tiles, all_total, BF16, "down_a")
    b_part = smooth_down(b_tiles, all_total, BF16, "down_b")
    from_xy = over_xy(jnp.concatenate([a_part, b_part], axis=0))
    from_x = over_x(smooth_down(x_tiles, all_total, BF16, "down_x"))
    from_y = over_y(smooth_down(y_tiles, all_total, BF16, "down_y"))
    own = smooth_down(own_tiles, all_total, F32, "down_own")

    return call(
        last_body,
        "last",
        [jax.ShapeDtypeStruct((rows, c), BF16), jax.ShapeDtypeStruct((rows, c), F32)],
        [tile_spec] * 5 + [whole((c, c))],
        [tile_spec] * 2,
        [own, from_x, from_y, from_xy, updated, w_out],
        grid=(steps,),
        flops=2 * rows * c * c,
    )


def solution(mesh):
    split = P(BOTH, None)
    return jax.shard_map(
        functools.partial(shards, mesh.shape["grp"], mesh.shape["dom"]),
        mesh=mesh,
        in_specs=(split, split, P(BOTH), P(BOTH)) + (P(),) * 8,
        out_specs=(split, split),
        check_vma=False,
    )
```

```python
import functools
import math

import jax
import jax.numpy as jnp
from jax import lax
from jax.experimental import pallas as pl
from jax.experimental.pallas import tpu as pltpu
from jax.sharding import PartitionSpec as P

BF16 = jnp.bfloat16
F32 = jnp.float32
BOTH = ("grp", "dom")
EPS = 1e-06
VMEM_LIMIT = 48 * 2**20


def dot(a, b, ca=1, cb=0):
    return lax.dot_general(a, b, (((ca,), (cb,)), ((), ())), preferred_element_type=F32)


def whole(shape):
    return pl.BlockSpec(shape, lambda *_: (0,) * len(shape))


def call(body, name, out_shape, in_specs, out_specs, args, grid=(1,), scratch=(), flops=0, exps=0, limit=VMEM_LIMIT):
    outs = out_shape if isinstance(out_shape, (list, tuple)) else [out_shape]
    moved = sum(a.size * a.dtype.itemsize for a in (*args, *outs))
    return pl.pallas_call(
        body,
        grid=grid,
        in_specs=in_specs,
        out_specs=out_specs,
        out_shape=out_shape,
        scratch_shapes=list(scratch),
        name=name,
        compiler_params=pltpu.CompilerParams(vmem_limit_bytes=limit),
        cost_estimate=pl.CostEstimate(flops=flops, bytes_accessed=moved, transcendentals=exps),
    )(*args)


def picked(ids, table):
    rows = table.shape[0]
    place = lax.broadcasted_iota(jnp.int32, (rows, ids.shape[1]), 0)
    hot = jnp.where(place == ids, 1.0, 0.0).astype(BF16)
    return dot(hot, table, 0, 0).astype(BF16)


def send_body(ids_ref, nodes_ref, prev_ref, next_ref):
    rows = picked(ids_ref[...], nodes_ref[...])
    half = rows.shape[0] // 2
    prev_ref[...] = rows[:half]
    next_ref[...] = rows[half:]


def hot_rows(ids, first, width):
    n = ids.shape[1]
    spread = jnp.transpose(jnp.broadcast_to(ids, (128, n)))
    lane = lax.broadcasted_iota(jnp.int32, (n, 128), 1)
    parts = [
        jnp.where(spread == lane + (first + 128 * c), 1.0, 0.0).astype(BF16)
        for c in range(width // 128)
    ]
    return jnp.concatenate(parts, axis=1)


def own_body(links_ref, nodes_ref, tile_ref, w_src_ref, w_dst_ref, bias_ref, pre_ref, source):
    @pl.when(pl.program_id(0) == 0)
    def _():
        source[...] = dot(nodes_ref[...], w_src_ref[...]).astype(BF16)

    target = dot(tile_ref[...], w_dst_ref[...]) + bias_ref[...]
    links = links_ref[...]
    for k in range(links.shape[0]):
        hot = hot_rows(links[k : k + 1], 0, source.shape[0])
        pre_ref[k] = dot(hot, source[...]) + target


def gelu(x):
    inner = math.sqrt(2.0 / math.pi) * (x + 0.044715 * (x * x * x))
    return 0.5 * x * (1.0 + jnp.tanh(inner))


def edge_body(
    links_ref,
    pre_ref,
    prev_ref,
    next_ref,
    tile_ref,
    ids_ref,
    w_src_ref,
    w_msg_ref,
    w_key_ref,
    w_query_ref,
    updated_ref,
    normed_ref,
    keys_ref,
    source,
    table,
):
    step = pl.program_id(0)
    halo = prev_ref.shape[0]
    rows = table.shape[0]

    @pl.when(step == 0)
    def _():
        source[:halo] = dot(prev_ref[...], w_src_ref[...]).astype(BF16)
        source[halo:] = dot(next_ref[...], w_src_ref[...]).astype(BF16)

    links = links_ref[...]
    count = links.shape[0]
    total = 0.0
    for k in range(count):
        hot = hot_rows(links[k : k + 1], rows, 2 * halo)
        total += gelu(pre_ref[k] + dot(hot, source[...]))
    messages = (total * (1.0 / count)).astype(BF16)
    updated = (tile_ref[...].astype(F32) + dot(messages, w_msg_ref[...])).astype(BF16)
    updated_ref[...] = updated
    wide = updated.astype(F32)
    normed = (wide * lax.rsqrt(jnp.mean(wide * wide, axis=1, keepdims=True) + EPS)).astype(BF16)
    normed_ref[...] = normed
    n = normed.shape[0]
    table[pl.ds(pl.multiple_of(step * n, n), n), :] = normed

    @pl.when(step == pl.num_programs(0) - 1)
    def _():
        keys = dot(picked(ids_ref[...], table[...]), w_key_ref[...]).astype(BF16)
        keys_ref[...] = dot(keys, w_query_ref[...], 1, 1).astype(BF16)


def smooth_up_body(count, scale, *refs):
    nodes, keys_ref, tiles, sums_ref = refs[:count], refs[count], refs[count + 1 : -1], refs[-1]
    total = 0.0
    for node_ref, tile_ref in zip(nodes, tiles):
        tile = jnp.exp2(dot(keys_ref[...], node_ref[...], 1, 1) * scale).astype(BF16)
        tile_ref[...] = tile
        total += dot(tile, node_ref[...])
    sums_ref[...] = total.astype(BF16)


def smooth_up(blocks, keys, name):
    marks, c = keys.shape
    step = min(marks, 512)
    scale = 2.0 * c ** (-0.5) * math.log2(math.e)
    sizes = [b.shape[0] for b in blocks]
    keys_spec = pl.BlockSpec((step, c), lambda j: (j, 0))
    out = call(
        functools.partial(smooth_up_body, len(blocks), scale),
        name,
        [jax.ShapeDtypeStruct((marks, n), BF16) for n in sizes]
        + [jax.ShapeDtypeStruct((marks, c), BF16)],
        [whole(b.shape) for b in blocks] + [keys_spec],
        [pl.BlockSpec((step, n), lambda j: (j, 0)) for n in sizes] + [keys_spec],
        [*blocks, keys],
        grid=(marks // step,),
        flops=4 * marks * sum(sizes) * c,
        exps=marks * sum(sizes),
    )
    return out[:-1], out[-1]


def smooth_down_body(count, *refs):
    tiles, sums, out_ref = refs[:count], refs[count:-1], refs[-1]
    total = 0.0
    for tile_ref, sum_ref in zip(tiles, sums):
        total += dot(tile_ref[...], sum_ref[...], 0, 0)
    out_ref[...] = total.astype(out_ref.dtype)


def smooth_down(tiles, sums, out_dtype, name):
    n = tiles[0].shape[1]
    c = sums[0].shape[1]
    step = min(n, 256)
    return call(
        functools.partial(smooth_down_body, len(tiles)),
        name,
        jax.ShapeDtypeStruct((n, c), out_dtype),
        [pl.BlockSpec((t.shape[0], step), lambda j: (0, j)) for t in tiles]
        + [whole(v.shape) for v in sums],
        pl.BlockSpec((step, c), lambda j: (j, 0)),
        [*tiles, *sums],
        grid=(n // step,),
        flops=sum(2 * t.shape[0] * n * c for t in tiles),
    )


def last_body(own_ref, xa_ref, ya_ref, yb_ref, xb_ref, updated_ref, w_out_ref, result_ref, term_ref):
    half = own_ref.shape[0] // 2
    for h, first, second in ((0, xa_ref, ya_ref), (1, yb_ref, xb_ref)):
        at = slice(h * half, (h + 1) * half)
        smooth = own_ref[at, :] + first[...].astype(F32) + second[...].astype(F32)
        term = smooth * lax.rsqrt(jnp.mean(smooth * smooth, axis=1, keepdims=True) + EPS)
        term_ref[at, :] = term
        result = updated_ref[at, :].astype(F32) + dot(term.astype(BF16), w_out_ref[...])
        result_ref[at, :] = result.astype(BF16)


def shards(
    groups,
    domains,
    nodes,
    neighbours,
    send_rows,
    landmark_ids,
    w_dst,
    w_src,
    w_msg,
    edge_bias,
    w_query,
    w_key,
    w_value,
    w_out,
):
    rows, c = nodes.shape
    halo = send_rows.shape[0] // 2
    mine = landmark_ids.shape[0]
    slots = neighbours.shape[1]
    line = domains // 2
    parts = groups * domains
    half = rows // 2

    def pair(axis, size, flip):
        return lambda v: lax.ppermute(v, axis, [(i, i ^ flip) for i in range(size)])

    over_core = pair("grp", groups, 1)
    over_x = pair("grp", groups, 2)
    over_y = pair("dom", domains, 1)
    over_z = [pair("dom", domains, 2 * t) for t in range(line)]
    to_prev, to_next = call(
        send_body,
        "send_rows",
        [jax.ShapeDtypeStruct((halo, c), BF16)] * 2,
        [whole((1, 2 * halo)), whole((rows, c))],
        [whole((halo, c))] * 2,
        [send_rows.reshape(1, 2 * halo), nodes],
        flops=4 * halo * rows * c,
    )
    from_prev = lax.ppermute(to_next, BOTH, [(i, (i + 1) % parts) for i in range(parts)])
    from_next = lax.ppermute(to_prev, BOTH, [((i + 1) % parts, i) for i in range(parts)])

    links = neighbours.T
    tile = min(rows, 256)
    steps = rows // tile
    links_spec = pl.BlockSpec((slots, tile), lambda i: (0, i))
    tile_spec = pl.BlockSpec((tile, c), lambda i: (i, 0))
    pre_spec = pl.BlockSpec((slots, tile, c), lambda i: (0, i, 0))
    pre = call(
        own_body,
        "own_edges",
        jax.ShapeDtypeStruct((slots, rows, c), F32),
        [links_spec, whole((rows, c)), tile_spec, whole((c, c)), whole((c, c)), whole((1, c))],
        pre_spec,
        [links, nodes, nodes, w_src, w_dst, edge_bias.reshape(1, c)],
        grid=(steps,),
        scratch=[pltpu.VMEM((rows, c), BF16)],
        flops=2 * slots * rows * rows * c,
    )
    updated, normed, keys = call(
        edge_body,
        "edges",
        [
            jax.ShapeDtypeStruct((rows, c), BF16),
            jax.ShapeDtypeStruct((rows, c), BF16),
            jax.ShapeDtypeStruct((mine, c), BF16),
        ],
        [
            links_spec,
            pre_spec,
            whole((halo, c)),
            whole((halo, c)),
            tile_spec,
            whole((1, mine)),
            whole((c, c)),
            whole((c, c)),
            whole((c, c)),
            whole((c, c)),
        ],
        [tile_spec, tile_spec, whole((mine, c))],
        [
            links,
            pre,
            from_prev,
            from_next,
            nodes,
            landmark_ids.reshape(1, mine),
            w_src,
            w_msg,
            w_key,
            w_query,
        ],
        grid=(steps,),
        scratch=[pltpu.VMEM((2 * halo, c), BF16), pltpu.VMEM((rows, c), BF16)],
        flops=4 * slots * rows * halo * c,
        exps=slots * rows * c,
    )

    x_a, y_b = over_x(normed[:half]), over_y(normed[half:])
    key_blocks = [keys] + [over_z[t](keys) for t in range(1, line)]
    x_b, y_a = over_x(normed[half:]), over_y(normed[:half])
    xy_a, xy_b = over_y(x_a), over_x(y_b)
    part = mine // 2
    side = line * part
    near = (normed, x_a, x_b, y_a, y_b)
    tiles = [[] for _ in range(7)]
    sums = []
    for h in range(2):
        side_keys = jnp.concatenate([k[h * part : (h + 1) * part] for k in key_blocks], axis=0)
        marks = jnp.concatenate([side_keys, over_core(side_keys)], axis=0)
        near_tiles, near_sums = smooth_up(near, marks, f"up_near_{h}")
        far_tiles, far_sums = smooth_up((xy_a, xy_b), marks, f"up_far_{h}")
        for held, tile in zip(tiles, [*near_tiles, *far_tiles]):
            held.append(tile)
        both = (near_sums.astype(F32) + far_sums.astype(F32)).astype(BF16)
        core_sums = (both[:side].astype(F32) + over_core(both[side:]).astype(F32)).astype(BF16)
        blocks = [core_sums[t * part : (t + 1) * part] for t in range(line)]
        total = blocks[0].astype(F32)
        for t in range(1, line):
            total = total + over_z[t](blocks[t]).astype(F32)
        total = dot(total.astype(BF16), w_value).astype(BF16)
        side_sums = jnp.concatenate([total] + [over_z[t](total) for t in range(1, line)], axis=0)
        sums.append(jnp.concatenate([side_sums, over_core(side_sums)], axis=0))

    def down(block, dtype, name):
        return smooth_down(tiles[block], sums, dtype, name)

    own_tiles, x_a_tiles, x_b_tiles, y_a_tiles, y_b_tiles, xy_a_tiles, xy_b_tiles = range(7)
    far_a = over_x(down(xy_a_tiles, BF16, "down_far_a"))
    far_b = over_y(down(xy_b_tiles, BF16, "down_far_b"))
    first_a = over_x(down(x_a_tiles, BF16, "down_x_a"))
    first_b = over_y(down(y_b_tiles, BF16, "down_y_b"))
    pass_a = down(y_a_tiles, F32, "down_y_a")
    pass_b = down(x_b_tiles, F32, "down_x_b")
    second_a = over_y((pass_a + far_a.astype(F32)).astype(BF16))
    second_b = over_x((pass_b + far_b.astype(F32)).astype(BF16))
    own = down(own_tiles, F32, "down_own")

    return call(
        last_body,
        "last",
        [jax.ShapeDtypeStruct((rows, c), BF16), jax.ShapeDtypeStruct((rows, c), F32)],
        [whole((rows, c))] + [whole((half, c))] * 4 + [whole((rows, c)), whole((c, c))],
        [whole((rows, c))] * 2,
        [own, first_a, second_a, first_b, second_b, updated, w_out],
        flops=2 * rows * c * c,
    )


def solution(mesh):
    split = P(BOTH, None)
    return jax.shard_map(
        functools.partial(shards, mesh.shape["grp"], mesh.shape["dom"]),
        mesh=mesh,
        in_specs=(split, split, P(BOTH), P(BOTH)) + (P(),) * 8,
        out_specs=(split, split),
        check_vma=False,
    )
```

```python
import functools
import math

import jax
import jax.numpy as jnp
from jax import lax
from jax.experimental import pallas as pl
from jax.experimental.pallas import tpu as pltpu
from jax.sharding import PartitionSpec as P

BF16 = jnp.bfloat16
F32 = jnp.float32
BOTH = ("grp", "dom")
EPS = 1e-06
VMEM_LIMIT = 24 * 2**20
WIDE_LIMIT = 62 * 2**20


def dot(a, b, ca=1, cb=0):
    return lax.dot_general(a, b, (((ca,), (cb,)), ((), ())), preferred_element_type=F32)


def whole(shape):
    return pl.BlockSpec(shape, lambda *_: (0,) * len(shape))


def call(body, name, out_shape, in_specs, out_specs, args, grid=(1,), scratch=(), cost=1, limit=VMEM_LIMIT):
    return pl.pallas_call(
        body,
        grid=grid,
        in_specs=in_specs,
        out_specs=out_specs,
        out_shape=out_shape,
        scratch_shapes=list(scratch),
        name=name,
        compiler_params=pltpu.CompilerParams(vmem_limit_bytes=limit),
        cost_estimate=pl.CostEstimate(flops=cost, bytes_accessed=1, transcendentals=0),
    )(*args)


def picked(ids, table):
    rows = table.shape[0]
    place = lax.broadcasted_iota(jnp.int32, (rows, ids.shape[1]), 0)
    hot = jnp.where(place == ids, 1.0, 0.0).astype(BF16)
    return dot(hot, table, 0, 0).astype(BF16)


def send_body(ids_ref, nodes_ref, prev_ref, next_ref):
    rows = picked(ids_ref[...], nodes_ref[...])
    half = rows.shape[0] // 2
    prev_ref[...] = rows[:half]
    next_ref[...] = rows[half:]


def hot_rows(ids, first, width):
    n = ids.shape[1]
    spread = jnp.transpose(jnp.broadcast_to(ids, (128, n)))
    lane = lax.broadcasted_iota(jnp.int32, (n, 128), 1)
    parts = [
        jnp.where(spread == lane + (first + 128 * c), 1.0, 0.0).astype(BF16)
        for c in range(width // 128)
    ]
    return jnp.concatenate(parts, axis=1)


def own_body(links_ref, nodes_ref, tile_ref, w_src_ref, w_dst_ref, bias_ref, pre_ref, source):
    @pl.when(pl.program_id(0) == 0)
    def _():
        source[...] = dot(nodes_ref[...], w_src_ref[...]).astype(BF16)

    target = dot(tile_ref[...], w_dst_ref[...]) + bias_ref[...]
    links = links_ref[...]
    for k in range(links.shape[0]):
        hot = hot_rows(links[k : k + 1], 0, source.shape[0])
        pre_ref[k] = dot(hot, source[...]) + target


def gelu(x):
    inner = math.sqrt(2.0 / math.pi) * (x + 0.044715 * (x * x * x))
    return 0.5 * x * (1.0 + jnp.tanh(inner))


def edge_body(
    links_ref,
    pre_ref,
    prev_ref,
    next_ref,
    tile_ref,
    ids_ref,
    w_src_ref,
    w_msg_ref,
    w_key_ref,
    w_query_ref,
    updated_ref,
    normed_ref,
    keys_ref,
    source,
    table,
):
    step = pl.program_id(0)
    halo = prev_ref.shape[0]
    rows = table.shape[0]

    @pl.when(step == 0)
    def _():
        source[:halo] = dot(prev_ref[...], w_src_ref[...]).astype(BF16)
        source[halo:] = dot(next_ref[...], w_src_ref[...]).astype(BF16)

    links = links_ref[...]
    count = links.shape[0]
    total = 0.0
    for k in range(count):
        hot = hot_rows(links[k : k + 1], rows, 2 * halo)
        total += gelu(pre_ref[k] + dot(hot, source[...]))
    messages = (total * (1.0 / count)).astype(BF16)
    updated = (tile_ref[...].astype(F32) + dot(messages, w_msg_ref[...])).astype(BF16)
    updated_ref[...] = updated
    wide = updated.astype(F32)
    normed = (wide * lax.rsqrt(jnp.mean(wide * wide, axis=1, keepdims=True) + EPS)).astype(BF16)
    normed_ref[...] = normed
    n = normed.shape[0]
    table[pl.ds(pl.multiple_of(step * n, n), n), :] = normed

    @pl.when(step == pl.num_programs(0) - 1)
    def _():
        keys = dot(picked(ids_ref[...], table[...]), w_key_ref[...]).astype(BF16)
        keys_ref[...] = dot(keys, w_query_ref[...], 1, 1).astype(BF16)


def smooth_up_body(count, starts, scale, *refs):
    nodes, (side_ref, other_ref), refs = refs[:count], refs[count : count + 2], refs[count + 2 :]
    tiles = refs[starts:-1]
    keys = jnp.where(pl.program_id(0) % 2 == 0, side_ref[...], other_ref[...])
    total = 0.0
    for start_ref in refs[:starts]:
        total += start_ref[...].astype(F32)
    for node_ref, tile_ref in zip(nodes, tiles):
        tile = jnp.exp2(dot(keys, node_ref[...], 1, 1) * scale).astype(BF16)
        tile_ref[...] = tile
        total += dot(tile, node_ref[...])
    refs[-1][...] = total.astype(BF16)


def smooth_up(blocks, side_keys, other_keys, starts, halves, name):
    step, c = side_keys.shape[0] // 2, side_keys.shape[1]
    scale = 2.0 * c ** (-0.5) * math.log2(math.e)
    sizes = [b.shape[0] for b in blocks]
    marks = 2 * step * len(halves)
    first = halves[0]
    keys_spec = pl.BlockSpec((step, c), lambda j: (first + j // 2, 0))
    out = call(
        functools.partial(smooth_up_body, len(blocks), len(starts), scale),
        name,
        [jax.ShapeDtypeStruct((marks, n), BF16) for n in sizes]
        + [jax.ShapeDtypeStruct((marks, c), BF16)],
        [whole(b.shape) for b in blocks]
        + [keys_spec] * 2
        + [pl.BlockSpec((step, c), lambda j: (j, 0))] * len(starts),
        [pl.BlockSpec((step, n), lambda j: (j, 0)) for n in sizes]
        + [pl.BlockSpec((step, c), lambda j: (j, 0))],
        [*blocks, side_keys, other_keys, *starts],
        grid=(marks // step,),
        cost=4 * marks * sum(sizes) * c,
    )
    return out[:-1], out[-1]


def smooth_down_body(jobs, halves, *refs):
    tiles, sums, outs = refs[: -len(jobs) - halves], refs[-len(jobs) - halves : -len(jobs)], refs[-len(jobs) :]
    for (first, count), out_ref in zip(jobs, outs):
        total = 0.0
        for h, sum_ref in enumerate(sums):
            marks = sum_ref.shape[0]
            if count == 1:
                tile = tiles[first][h * marks : (h + 1) * marks, :]
            else:
                tile = tiles[first + h][...]
            total += dot(tile, sum_ref[...], 0, 0)
        out_ref[...] = total.astype(out_ref.dtype)


def smooth_down(jobs, sums, n, name):
    c = sums[0].shape[1]
    step = min(n, 256)
    tiles, specs, where = [], [], []
    for held, at, _ in jobs:
        where.append((len(tiles), len(held)))
        for tile in held:
            tiles.append(tile)
            specs.append(pl.BlockSpec((tile.shape[0], step), lambda j, at=at: (0, at // step + j)))
    return call(
        functools.partial(smooth_down_body, where, len(sums)),
        name,
        [jax.ShapeDtypeStruct((n, c), dtype) for _, _, dtype in jobs],
        specs + [whole(v.shape) for v in sums],
        [pl.BlockSpec((step, c), lambda j: (j, 0))] * len(jobs),
        [*tiles, *sums],
        grid=(n // step,),
    )


def last_body(own_ref, xa_ref, ya_ref, yb_ref, xb_ref, updated_ref, w_out_ref, result_ref, term_ref):
    half = own_ref.shape[0] // 2
    for h, first, second in ((0, xa_ref, ya_ref), (1, yb_ref, xb_ref)):
        at = slice(h * half, (h + 1) * half)
        smooth = own_ref[at, :] + first[...].astype(F32) + second[...].astype(F32)
        term = smooth * lax.rsqrt(jnp.mean(smooth * smooth, axis=1, keepdims=True) + EPS)
        term_ref[at, :] = term
        result = updated_ref[at, :].astype(F32) + dot(term.astype(BF16), w_out_ref[...])
        result_ref[at, :] = result.astype(BF16)


def shards(
    groups,
    domains,
    nodes,
    neighbours,
    send_rows,
    landmark_ids,
    w_dst,
    w_src,
    w_msg,
    edge_bias,
    w_query,
    w_key,
    w_value,
    w_out,
):
    rows, c = nodes.shape
    halo = send_rows.shape[0] // 2
    mine = landmark_ids.shape[0]
    slots = neighbours.shape[1]
    line = domains // 2
    parts = groups * domains
    half = rows // 2

    def pair(axis, size, flip):
        return lambda v: lax.ppermute(v, axis, [(i, i ^ flip) for i in range(size)])

    over_core = pair("grp", groups, 1)
    over_x = pair("grp", groups, 2)
    over_y = pair("dom", domains, 1)
    over_z = [pair("dom", domains, 2 * t) for t in range(line)]
    to_prev, to_next = call(
        send_body,
        "send_rows",
        [jax.ShapeDtypeStruct((halo, c), BF16)] * 2,
        [whole((1, 2 * halo)), whole((rows, c))],
        [whole((halo, c))] * 2,
        [send_rows.reshape(1, 2 * halo), nodes],
        limit=WIDE_LIMIT,
    )
    from_prev = lax.ppermute(to_next, BOTH, [(i, (i + 1) % parts) for i in range(parts)])
    from_next = lax.ppermute(to_prev, BOTH, [((i + 1) % parts, i) for i in range(parts)])

    links = neighbours.T
    tile = min(rows, 256)
    steps = rows // tile
    links_spec = pl.BlockSpec((slots, tile), lambda i: (0, i))
    tile_spec = pl.BlockSpec((tile, c), lambda i: (i, 0))
    pre_spec = pl.BlockSpec((slots, tile, c), lambda i: (0, i, 0))
    pre = call(
        own_body,
        "own_edges",
        jax.ShapeDtypeStruct((slots, rows, c), F32),
        [links_spec, whole((rows, c)), tile_spec, whole((c, c)), whole((c, c)), whole((1, c))],
        pre_spec,
        [links, nodes, nodes, w_src, w_dst, edge_bias.reshape(1, c)],
        grid=(steps,),
        scratch=[pltpu.VMEM((rows, c), BF16)],
        limit=WIDE_LIMIT,
    )
    updated, normed, keys = call(
        edge_body,
        "edges",
        [
            jax.ShapeDtypeStruct((rows, c), BF16),
            jax.ShapeDtypeStruct((rows, c), BF16),
            jax.ShapeDtypeStruct((mine, c), BF16),
        ],
        [
            links_spec,
            pre_spec,
            whole((halo, c)),
            whole((halo, c)),
            tile_spec,
            whole((1, mine)),
            whole((c, c)),
            whole((c, c)),
            whole((c, c)),
            whole((c, c)),
        ],
        [tile_spec, tile_spec, whole((mine, c))],
        [
            links,
            pre,
            from_prev,
            from_next,
            nodes,
            landmark_ids.reshape(1, mine),
            w_src,
            w_msg,
            w_key,
            w_query,
        ],
        grid=(steps,),
        scratch=[pltpu.VMEM((2 * halo, c), BF16), pltpu.VMEM((rows, c), BF16)],
        limit=WIDE_LIMIT,
    )

    part = mine // 2
    side = line * part
    key_blocks = [keys] + [over_z[t](keys) for t in range(1, line)]
    from_x, from_y = over_x(normed), over_y(normed)
    *key_blocks, from_x, from_y = lax.optimization_barrier((*key_blocks, from_x, from_y))
    xy_a, xy_b = over_y(from_x[:half]), over_x(from_y[half:])
    side_keys = jnp.concatenate(
        [k[h * part : (h + 1) * part] for h in range(2) for k in key_blocks], axis=0
    )
    other_keys = over_core(side_keys)
    own_tiles, own_sums = smooth_up([normed], side_keys, other_keys, (), (0, 1), "up_own")
    x_tiles, y_tiles, far_a_tiles, far_b_tiles, sums = [], [], [], [], []
    both = own_sums
    for h in range(2):
        from_x, from_y, _ = lax.optimization_barrier((from_x, from_y, both))
        (x_half, y_half), near_sums = smooth_up(
            [from_x, from_y], side_keys, other_keys, (), (h,), f"up_near_{h}"
        )
        (a_half, b_half), both = smooth_up(
            [xy_a, xy_b],
            side_keys,
            other_keys,
            (own_sums[h * 2 * side : (h + 1) * 2 * side], near_sums),
            (h,),
            f"up_far_{h}",
        )
        for held, tile in zip(
            (x_tiles, y_tiles, far_a_tiles, far_b_tiles), (x_half, y_half, a_half, b_half)
        ):
            held.append(tile)
        core_sums = (both[:side].astype(F32) + over_core(both[side:]).astype(F32)).astype(BF16)
        blocks = [core_sums[t * part : (t + 1) * part] for t in range(line)]
        total = blocks[0].astype(F32)
        for t in range(1, line):
            total = total + over_z[t](blocks[t]).astype(F32)
        total = dot(total.astype(BF16), w_value).astype(BF16)
        side_sums = jnp.concatenate([total] + [over_z[t](total) for t in range(1, line)], axis=0)
        sums.append(jnp.concatenate([side_sums, over_core(side_sums)], axis=0))

    far_a, far_b = smooth_down(
        [(far_a_tiles, 0, BF16), (far_b_tiles, 0, BF16)], sums, half, "down_far"
    )
    sums_0, sums_1, far_a, far_b = lax.optimization_barrier((*sums, far_a, far_b))
    sums = [sums_0, sums_1]
    first_a, first_b, pass_a, pass_b = smooth_down(
        [
            (x_tiles, 0, BF16),
            (y_tiles, half, BF16),
            (y_tiles, 0, F32),
            (x_tiles, half, F32),
        ],
        sums,
        half,
        "down_near",
    )
    far_a, far_b = over_x(far_a), over_y(far_b)
    first_a, first_b = over_x(first_a), over_y(first_b)
    second_a = over_y((pass_a + far_a.astype(F32)).astype(BF16))
    second_b = over_x((pass_b + far_b.astype(F32)).astype(BF16))
    (own,) = smooth_down([(own_tiles, 0, F32)], sums, rows, "down_own")

    return call(
        last_body,
        "last",
        [jax.ShapeDtypeStruct((rows, c), BF16), jax.ShapeDtypeStruct((rows, c), F32)],
        [whole((rows, c))] + [whole((half, c))] * 4 + [whole((rows, c)), whole((c, c))],
        [whole((rows, c))] * 2,
        [own, first_a, second_a, first_b, second_b, updated, w_out],
    )


def solution(mesh):
    split = P(BOTH, None)
    return jax.shard_map(
        functools.partial(shards, mesh.shape["grp"], mesh.shape["dom"]),
        mesh=mesh,
        in_specs=(split, split, P(BOTH), P(BOTH)) + (P(),) * 8,
        out_specs=(split, split),
        check_vma=False,
    )
```

```python
import functools
import math

import jax
import jax.numpy as jnp
from jax import lax
from jax.experimental import pallas as pl
from jax.experimental.pallas import tpu as pltpu
from jax.sharding import PartitionSpec as P

BF16 = jnp.bfloat16
F32 = jnp.float32
BOTH = ("grp", "dom")
EPS = 1e-06
VMEM_LIMIT = 24 * 2**20
WIDE_LIMIT = 62 * 2**20


def dot(a, b, ca=1, cb=0):
    return lax.dot_general(a, b, (((ca,), (cb,)), ((), ())), preferred_element_type=F32)


def whole(shape):
    return pl.BlockSpec(shape, lambda *_: (0,) * len(shape))


def call(body, name, out_shape, in_specs, out_specs, args, grid=(1,), scratch=(), cost=1, limit=VMEM_LIMIT):
    return pl.pallas_call(
        body,
        grid=grid,
        in_specs=in_specs,
        out_specs=out_specs,
        out_shape=out_shape,
        scratch_shapes=list(scratch),
        name=name,
        compiler_params=pltpu.CompilerParams(vmem_limit_bytes=limit),
        cost_estimate=pl.CostEstimate(flops=cost, bytes_accessed=1, transcendentals=0),
    )(*args)


def picked(ids, table):
    rows = table.shape[0]
    place = lax.broadcasted_iota(jnp.int32, (rows, ids.shape[1]), 0)
    hot = jnp.where(place == ids, 1.0, 0.0).astype(BF16)
    return dot(hot, table, 0, 0).astype(BF16)


def send_body(ids_ref, nodes_ref, prev_ref, next_ref):
    rows = picked(ids_ref[...], nodes_ref[...])
    half = rows.shape[0] // 2
    prev_ref[...] = rows[:half]
    next_ref[...] = rows[half:]


def hot_rows(ids, first, width):
    n = ids.shape[1]
    spread = jnp.transpose(jnp.broadcast_to(ids, (128, n)))
    lane = lax.broadcasted_iota(jnp.int32, (n, 128), 1)
    parts = [
        jnp.where(spread == lane + (first + 128 * c), 1.0, 0.0).astype(BF16)
        for c in range(width // 128)
    ]
    return jnp.concatenate(parts, axis=1)


def own_body(links_ref, nodes_ref, tile_ref, w_src_ref, w_dst_ref, bias_ref, pre_ref, source):
    @pl.when(pl.program_id(0) == 0)
    def _():
        source[...] = dot(nodes_ref[...], w_src_ref[...]).astype(BF16)

    target = dot(tile_ref[...], w_dst_ref[...]) + bias_ref[...]
    links = links_ref[...]
    for k in range(links.shape[0]):
        hot = hot_rows(links[k : k + 1], 0, source.shape[0])
        pre_ref[k] = dot(hot, source[...]) + target


def gelu(x):
    inner = math.sqrt(2.0 / math.pi) * (x + 0.044715 * (x * x * x))
    return 0.5 * x * (1.0 + jnp.tanh(inner))


def edge_body(
    links_ref,
    pre_ref,
    prev_ref,
    next_ref,
    tile_ref,
    ids_ref,
    w_src_ref,
    w_msg_ref,
    w_key_ref,
    w_query_ref,
    updated_ref,
    normed_ref,
    keys_ref,
    source,
    table,
):
    step = pl.program_id(0)
    halo = prev_ref.shape[0]
    rows = table.shape[0]

    @pl.when(step == 0)
    def _():
        source[:halo] = dot(prev_ref[...], w_src_ref[...]).astype(BF16)
        source[halo:] = dot(next_ref[...], w_src_ref[...]).astype(BF16)

    links = links_ref[...]
    count = links.shape[0]
    total = 0.0
    for k in range(count):
        hot = hot_rows(links[k : k + 1], rows, 2 * halo)
        total += gelu(pre_ref[k] + dot(hot, source[...]))
    messages = (total * (1.0 / count)).astype(BF16)
    updated = (tile_ref[...].astype(F32) + dot(messages, w_msg_ref[...])).astype(BF16)
    updated_ref[...] = updated
    wide = updated.astype(F32)
    normed = (wide * lax.rsqrt(jnp.mean(wide * wide, axis=1, keepdims=True) + EPS)).astype(BF16)
    normed_ref[...] = normed
    n = normed.shape[0]
    table[pl.ds(pl.multiple_of(step * n, n), n), :] = normed

    @pl.when(step == pl.num_programs(0) - 1)
    def _():
        keys = dot(picked(ids_ref[...], table[...]), w_key_ref[...]).astype(BF16)
        keys_ref[...] = dot(keys, w_query_ref[...], 1, 1).astype(BF16)


def smooth_up_body(count, groups, starts, scale, *refs):
    nodes, keys, refs = refs[:count], refs[count : count + groups], refs[count + groups :]
    (sums_ref, held), tiles = refs[-2:], refs[starts:-2]
    step = sums_ref.shape[0]

    @pl.when(pl.program_id(0) == 0)
    def _():
        first = 0
        for key_ref in keys:
            held[first : first + key_ref.shape[0], :] = key_ref[...]
            first += key_ref.shape[0]

    marks = held[pl.ds(pl.multiple_of(pl.program_id(0) * step, step), step), :]
    total = 0.0
    for start_ref in refs[:starts]:
        total += start_ref[...].astype(F32)
    for node_ref, tile_ref in zip(nodes, tiles):
        tile = jnp.exp2(dot(marks, node_ref[...], 1, 1) * scale).astype(BF16)
        tile_ref[...] = tile
        total += dot(tile, node_ref[...])
    sums_ref[...] = total.astype(BF16)


def smooth_up(blocks, keys, starts, name):
    marks, c = sum(k.shape[0] for k in keys), keys[0].shape[1]
    step = min(marks, 512)
    scale = 2.0 * c ** (-0.5) * math.log2(math.e)
    sizes = [b.shape[0] for b in blocks]
    rows_spec = pl.BlockSpec((step, c), lambda j: (j, 0))
    out = call(
        functools.partial(smooth_up_body, len(blocks), len(keys), len(starts), scale),
        name,
        [jax.ShapeDtypeStruct((marks, n), BF16) for n in sizes]
        + [jax.ShapeDtypeStruct((marks, c), BF16)],
        [whole(v.shape) for v in (*blocks, *keys)] + [rows_spec] * len(starts),
        [pl.BlockSpec((step, n), lambda j: (j, 0)) for n in sizes] + [rows_spec],
        [*blocks, *keys, *starts],
        grid=(marks // step,),
        scratch=[pltpu.VMEM((marks, c), BF16)],
        cost=marks * sum(sizes) * c,
    )
    return out[:-1], out[-1]


def smooth_down_body(count, halves, starts, *refs):
    tiles, sums = refs[: 2 * count], refs[2 * count : 2 * count + 2 * halves]
    begun, outs = refs[2 * count + 2 * halves : -count], refs[-count:]
    for b, out_ref in enumerate(outs):
        total = begun[b][...] if starts else 0.0
        for side, tile_ref in enumerate(tiles[2 * b : 2 * b + 2]):
            line, mine, n = tile_ref.shape
            part = mine // halves
            for h in range(halves):
                tile = tile_ref[:, h * part : (h + 1) * part, :].reshape(line * part, n)
                total += dot(tile, sums[2 * h + side][...], 0, 0)
        out_ref[...] = total.astype(out_ref.dtype)


def smooth_down(jobs, sums, n, name, half=None, starts=()):
    c = sums[0].shape[1]
    step = min(n, 256)
    rows_spec = pl.BlockSpec((step, c), lambda j: (j, 0))
    args, specs = [], []
    for tiles, at, _ in jobs:
        for tile in tiles:
            line, mine, _ = tile.shape
            args.append(tile)
            if half is None:
                shape, place = (line, mine, step), 0
            else:
                shape, place = (line, mine // 2, step), half
            specs.append(pl.BlockSpec(shape, lambda j, at=at, place=place: (0, place, at // step + j)))
    return call(
        functools.partial(smooth_down_body, len(jobs), len(sums) // 2, len(starts)),
        name,
        [jax.ShapeDtypeStruct((n, c), dtype) for _, _, dtype in jobs],
        specs + [whole(v.shape) for v in sums] + [rows_spec] * len(starts),
        [rows_spec] * len(jobs),
        [*args, *sums, *starts],
        grid=(n // step,),
    )


def last_body(own_ref, xa_ref, ya_ref, yb_ref, xb_ref, updated_ref, w_out_ref, result_ref, term_ref):
    half = own_ref.shape[0] // 2
    for h, first, second in ((0, xa_ref, ya_ref), (1, yb_ref, xb_ref)):
        at = slice(h * half, (h + 1) * half)
        smooth = own_ref[at, :] + first[...].astype(F32) + second[...].astype(F32)
        term = smooth * lax.rsqrt(jnp.mean(smooth * smooth, axis=1, keepdims=True) + EPS)
        term_ref[at, :] = term
        result = updated_ref[at, :].astype(F32) + dot(term.astype(BF16), w_out_ref[...])
        result_ref[at, :] = result.astype(BF16)


def shards(
    groups,
    domains,
    nodes,
    neighbours,
    send_rows,
    landmark_ids,
    w_dst,
    w_src,
    w_msg,
    edge_bias,
    w_query,
    w_key,
    w_value,
    w_out,
):
    rows, c = nodes.shape
    halo = send_rows.shape[0] // 2
    mine = landmark_ids.shape[0]
    slots = neighbours.shape[1]
    line = domains // 2
    parts = groups * domains
    half = rows // 2

    def pair(axis, size, flip):
        return lambda v: lax.ppermute(v, axis, [(i, i ^ flip) for i in range(size)])

    over_core = pair("grp", groups, 1)
    over_x = pair("grp", groups, 2)
    over_y = pair("dom", domains, 1)
    over_z = [pair("dom", domains, 2 * t) for t in range(line)]
    to_prev, to_next = call(
        send_body,
        "send_rows",
        [jax.ShapeDtypeStruct((halo, c), BF16)] * 2,
        [whole((1, 2 * halo)), whole((rows, c))],
        [whole((halo, c))] * 2,
        [send_rows.reshape(1, 2 * halo), nodes],
        limit=WIDE_LIMIT,
    )
    from_prev = lax.ppermute(to_next, BOTH, [(i, (i + 1) % parts) for i in range(parts)])
    from_next = lax.ppermute(to_prev, BOTH, [((i + 1) % parts, i) for i in range(parts)])

    links = neighbours.T
    tile = min(rows, 256)
    steps = rows // tile
    links_spec = pl.BlockSpec((slots, tile), lambda i: (0, i))
    tile_spec = pl.BlockSpec((tile, c), lambda i: (i, 0))
    pre_spec = pl.BlockSpec((slots, tile, c), lambda i: (0, i, 0))
    pre = call(
        own_body,
        "own_edges",
        jax.ShapeDtypeStruct((slots, rows, c), F32),
        [links_spec, whole((rows, c)), tile_spec, whole((c, c)), whole((c, c)), whole((1, c))],
        pre_spec,
        [links, nodes, nodes, w_src, w_dst, edge_bias.reshape(1, c)],
        grid=(steps,),
        scratch=[pltpu.VMEM((rows, c), BF16)],
        limit=WIDE_LIMIT,
    )
    updated, normed, keys = call(
        edge_body,
        "edges",
        [
            jax.ShapeDtypeStruct((rows, c), BF16),
            jax.ShapeDtypeStruct((rows, c), BF16),
            jax.ShapeDtypeStruct((mine, c), BF16),
        ],
        [
            links_spec,
            pre_spec,
            whole((halo, c)),
            whole((halo, c)),
            tile_spec,
            whole((1, mine)),
            whole((c, c)),
            whole((c, c)),
            whole((c, c)),
            whole((c, c)),
        ],
        [tile_spec, tile_spec, whole((mine, c))],
        [
            links,
            pre,
            from_prev,
            from_next,
            nodes,
            landmark_ids.reshape(1, mine),
            w_src,
            w_msg,
            w_key,
            w_query,
        ],
        grid=(steps,),
        scratch=[pltpu.VMEM((2 * halo, c), BF16), pltpu.VMEM((rows, c), BF16)],
        limit=WIDE_LIMIT,
    )

    key_blocks = [keys] + [over_z[t](keys) for t in range(1, line)]
    from_x, from_y = over_x(normed), over_y(normed)
    *key_blocks, from_x, from_y = lax.optimization_barrier((*key_blocks, from_x, from_y))
    other_keys = [over_core(jnp.concatenate(key_blocks, axis=0))]
    far = (over_y(from_x[:half]), over_x(from_y[half:]))
    near = (normed, from_x, from_y)
    near_side, side_sums = smooth_up(near, key_blocks, (), "up_near_side")
    *near, side_sums = lax.optimization_barrier((*near, side_sums))
    near_other, other_sums = smooth_up(near, other_keys, (), "up_near_other")
    far_other, other_sums = smooth_up(far, other_keys, (other_sums,), "up_far_other")
    *far, other_sums = lax.optimization_barrier((*far, other_sums))
    far_side, side_sums = smooth_up(far, key_blocks, (side_sums,), "up_far_side")
    core_sums = (side_sums.astype(F32) + over_core(other_sums).astype(F32)).astype(BF16)

    part = mine // 2
    sums = []
    for h in range(2):
        blocks = [core_sums[t * mine + h * part : t * mine + (h + 1) * part] for t in range(line)]
        total = blocks[0].astype(F32)
        for t in range(1, line):
            total = total + over_z[t](blocks[t]).astype(F32)
        total = dot(total.astype(BF16), w_value).astype(BF16)
        side = jnp.concatenate([total] + [over_z[t](total) for t in range(1, line)], axis=0)
        sums.append((side, over_core(side)))

    tiles = [
        tuple(v.reshape(line, mine, v.shape[1]) for v in pair)
        for pair in zip((*near_side, *far_side), (*near_other, *far_other))
    ]
    own_tiles, x_tiles, y_tiles, a_tiles, b_tiles = tiles
    far_jobs = [(a_tiles, 0), (b_tiles, 0)]
    near_jobs = [(x_tiles, 0), (y_tiles, half), (y_tiles, 0), (x_tiles, half)]
    begun = smooth_down([(*j, F32) for j in far_jobs], sums[0], half, "down_far_first", 0)
    far_a, far_b = smooth_down([(*j, BF16) for j in far_jobs], sums[1], half, "down_far", 1, begun)
    *both, far_a, far_b = lax.optimization_barrier((*sums[0], *sums[1], far_a, far_b))
    first_a, first_b, pass_a, pass_b = smooth_down(
        [(*j, dtype) for j, dtype in zip(near_jobs, (BF16, BF16, F32, F32))], both, half, "down_near"
    )
    far_a, far_b = over_x(far_a), over_y(far_b)
    first_a, first_b = over_x(first_a), over_y(first_b)
    second_a = over_y((pass_a + far_a.astype(F32)).astype(BF16))
    second_b = over_x((pass_b + far_b.astype(F32)).astype(BF16))
    (own,) = smooth_down([(own_tiles, 0, F32)], both, rows, "down_own")

    return call(
        last_body,
        "last",
        [jax.ShapeDtypeStruct((rows, c), BF16), jax.ShapeDtypeStruct((rows, c), F32)],
        [whole((rows, c))] + [whole((half, c))] * 4 + [whole((rows, c)), whole((c, c))],
        [whole((rows, c))] * 2,
        [own, first_a, second_a, first_b, second_b, updated, w_out],
    )


def solution(mesh):
    split = P(BOTH, None)
    return jax.shard_map(
        functools.partial(shards, mesh.shape["grp"], mesh.shape["dom"]),
        mesh=mesh,
        in_specs=(split, split, P(BOTH), P(BOTH)) + (P(),) * 8,
        out_specs=(split, split),
        check_vma=False,
    )
```

```python
import functools
import math

import jax
import jax.numpy as jnp
from jax import lax
from jax.experimental import pallas as pl
from jax.experimental.pallas import tpu as pltpu
from jax.sharding import PartitionSpec as P

BF16 = jnp.bfloat16
F32 = jnp.float32
BOTH = ("grp", "dom")
EPS = 1e-06
VMEM_LIMIT = 24 * 2**20


def dot(a, b, ca=1, cb=0):
    return lax.dot_general(a, b, (((ca,), (cb,)), ((), ())), preferred_element_type=F32)


def whole(shape):
    return pl.BlockSpec(shape, lambda *_: (0,) * len(shape))


def call(body, name, out_shape, in_specs, out_specs, args, grid=(1,), scratch=(), cost=1, limit=VMEM_LIMIT):
    return pl.pallas_call(
        body,
        grid=grid,
        in_specs=in_specs,
        out_specs=out_specs,
        out_shape=out_shape,
        scratch_shapes=list(scratch),
        name=name,
        compiler_params=pltpu.CompilerParams(vmem_limit_bytes=limit),
        cost_estimate=pl.CostEstimate(flops=cost, bytes_accessed=1, transcendentals=0),
    )(*args)


VMEM = pl.BlockSpec(memory_space=pltpu.VMEM)
HBM = pl.BlockSpec(memory_space=pltpu.HBM)


def call_flat(body, name, out_shape, args, in_specs=None, scratch=(), cost=1, limit=VMEM_LIMIT):
    return pl.pallas_call(
        body,
        in_specs=in_specs or [VMEM] * len(args),
        out_specs=[VMEM] * len(out_shape),
        out_shape=out_shape,
        scratch_shapes=list(scratch),
        name=name,
        compiler_params=pltpu.CompilerParams(vmem_limit_bytes=limit),
        cost_estimate=pl.CostEstimate(flops=cost, bytes_accessed=1, transcendentals=0),
    )(*args)


def picked(ids, table):
    rows = table.shape[0]
    place = lax.broadcasted_iota(jnp.int32, (rows, ids.shape[1]), 0)
    hot = jnp.where(place == ids, 1.0, 0.0).astype(BF16)
    return dot(hot, table, 0, 0).astype(BF16)


def send_body(count, *refs):
    given, (twin_ref, rest_ref), kept = refs[:count], refs[count : count + 2], refs[count + 2 : -2]
    ids, arrived = refs[-2:]
    copies = [
        pltpu.make_async_copy(src, dst, arrived.at[i])
        for i, (src, dst) in enumerate(zip(given, (ids, *kept)))
    ]
    for copy in copies:
        copy.start()
    copies[0].wait()
    copies[1].wait()
    rows = picked(ids[...], kept[0][...])
    half = rows.shape[0] // 2
    odd = lax.rem(lax.axis_index("dom"), 2) == 1
    twin_ref[...] = jnp.where(odd, rows[:half], rows[half:])
    rest_ref[...] = jnp.where(odd, rows[half:], rows[:half])
    for copy in copies[2:]:
        copy.wait()


def hot_rows(ids, first, width):
    n = ids.shape[1]
    spread = jnp.transpose(jnp.broadcast_to(ids, (128, n)))
    lane = lax.broadcasted_iota(jnp.int32, (n, 128), 1)
    parts = [
        jnp.where(spread == lane + (first + 128 * c), 1.0, 0.0).astype(BF16)
        for c in range(width // 128)
    ]
    return jnp.concatenate(parts, axis=1)


def own_body(nodes, w_src, links, w_dst, bias, pre_ref, source):
    source[...] = dot(nodes[...], w_src[...]).astype(BF16)
    slots, rows = links.shape
    tile = min(rows, 256)
    for first in range(0, rows, tile):
        at = slice(first, first + tile)
        target = dot(nodes[at, :], w_dst[...]) + bias[...]
        for k in range(slots):
            hot = hot_rows(links[k : k + 1, at], 0, rows)
            pre_ref[k, at, :] = dot(hot, source[...]) + target


def twice_gelu(x):
    slope = math.sqrt(2.0 / math.pi)
    return x * (1.0 + jnp.tanh(x * (slope + (0.044715 * slope) * (x * x))))


def edge_body(
    nodes,
    w_src,
    links,
    ids,
    w_msg,
    w_key,
    w_query,
    pre,
    twin,
    rest,
    updated_ref,
    normed_ref,
    keys_ref,
    source,
):
    halo = twin.shape[0]
    slots, rows = links.shape
    odd = lax.rem(lax.axis_index("dom"), 2) == 1
    source[:halo] = dot(jnp.where(odd, twin[...], rest[...]), w_src[...]).astype(BF16)
    source[halo:] = dot(jnp.where(odd, rest[...], twin[...]), w_src[...]).astype(BF16)
    tile = min(rows, 256)
    for first in range(0, rows, tile):
        at = slice(first, first + tile)
        total = 0.0
        for k in range(slots):
            hot = hot_rows(links[k : k + 1, at], rows, 2 * halo)
            total += twice_gelu(pre[k, at, :] + dot(hot, source[...]))
        messages = (total * (0.5 / slots)).astype(BF16)
        updated = (nodes[at, :].astype(F32) + dot(messages, w_msg[...])).astype(BF16)
        updated_ref[at, :] = updated
        wide = updated.astype(F32)
        normed = wide * lax.rsqrt(jnp.mean(wide * wide, axis=1, keepdims=True) + EPS)
        normed_ref[at, :] = normed.astype(BF16)
    keys = dot(picked(ids[...], normed_ref[...]), w_key[...]).astype(BF16)
    keys_ref[...] = dot(keys, w_query[...], 1, 1).astype(BF16)


def smooth_up_body(count, groups, starts, scale, *refs):
    nodes, keys, refs = refs[:count], refs[count : count + groups], refs[count + groups :]
    (sums_ref, held), tiles = refs[-2:], refs[starts:-2]
    first = 0
    for key_ref in keys:
        held[first : first + key_ref.shape[0], :] = key_ref[...]
        first += key_ref.shape[0]
    step = min(first, 512)
    for first in range(0, first, step):
        at = slice(first, first + step)
        total = 0.0
        for start_ref in refs[:starts]:
            total += start_ref[at, :].astype(F32)
        for node_ref, tile_ref in zip(nodes, tiles):
            tile = jnp.exp2(dot(held[at, :], node_ref[...], 1, 1) * scale).astype(BF16)
            tile_ref[at, :] = tile
            total += dot(tile, node_ref[...])
        sums_ref[at, :] = total.astype(BF16)


def smooth_up(blocks, keys, starts, name):
    marks, c = sum(k.shape[0] for k in keys), keys[0].shape[1]
    sizes = [b.shape[0] for b in blocks]
    out = call_flat(
        functools.partial(
            smooth_up_body, len(blocks), len(keys), len(starts), 2.0 * c ** (-0.5) * math.log2(math.e)
        ),
        name,
        [jax.ShapeDtypeStruct((marks, n), BF16) for n in sizes]
        + [jax.ShapeDtypeStruct((marks, c), BF16)],
        [*blocks, *keys, *starts],
        scratch=[pltpu.VMEM((marks, c), BF16)],
        cost=marks * sum(sizes) * c,
    )
    return out[:-1], out[-1]


def smooth_down_body(places, n, halves, starts, *refs):
    count = len(places)
    tiles, sums = refs[: 2 * count], refs[2 * count : 2 * count + 2 * len(halves)]
    begun, outs = refs[2 * count + 2 * len(halves) : -count], refs[-count:]
    for b, out_ref in enumerate(outs):
        total = begun[b][...] if starts else 0.0
        for side, tile_ref in enumerate(tiles[2 * b : 2 * b + 2]):
            line, mine, _ = tile_ref.shape
            part = mine // 2
            for i, h in enumerate(halves):
                tile = tile_ref[:, h * part : (h + 1) * part, places[b] : places[b] + n]
                total += dot(tile.reshape(line * part, n), sums[2 * i + side][...], 0, 0)
        out_ref[...] = total.astype(out_ref.dtype)


def smooth_down(jobs, sums, n, name, halves=(0, 1), starts=()):
    c = sums[0].shape[1]
    return call_flat(
        functools.partial(smooth_down_body, [at for _, at, _ in jobs], n, halves, len(starts)),
        name,
        [jax.ShapeDtypeStruct((n, c), dtype) for _, _, dtype in jobs],
        [*(tile for tiles, _, _ in jobs for tile in tiles), *sums, *starts],
    )


def last_body(own_ref, xa_ref, ya_ref, yb_ref, xb_ref, updated_ref, w_out_ref, result_ref, term_ref):
    half = own_ref.shape[0] // 2
    for h, first, second in ((0, xa_ref, ya_ref), (1, yb_ref, xb_ref)):
        at = slice(h * half, (h + 1) * half)
        smooth = own_ref[at, :] + first[...].astype(F32) + second[...].astype(F32)
        term = smooth * lax.rsqrt(jnp.mean(smooth * smooth, axis=1, keepdims=True) + EPS)
        term_ref[at, :] = term
        result = updated_ref[at, :].astype(F32) + dot(term.astype(BF16), w_out_ref[...])
        result_ref[at, :] = result.astype(BF16)


def shards(
    groups,
    domains,
    nodes,
    neighbours,
    send_rows,
    landmark_ids,
    w_dst,
    w_src,
    w_msg,
    edge_bias,
    w_query,
    w_key,
    w_value,
    w_out,
):
    rows, c = nodes.shape
    halo = send_rows.shape[0] // 2
    mine = landmark_ids.shape[0]
    slots = neighbours.shape[1]
    line = domains // 2
    parts = groups * domains
    half = rows // 2

    def pair(axis, size, flip):
        return lambda v: lax.ppermute(v, axis, [(i, i ^ flip) for i in range(size)])

    over_core = pair("grp", groups, 1)
    over_x = pair("grp", groups, 2)
    over_y = pair("dom", domains, 1)
    over_z = [pair("dom", domains, 2 * t) for t in range(line)]
    given = [
        send_rows.reshape(1, 2 * halo),
        nodes,
        w_src,
        neighbours.T,
        w_dst,
        edge_bias.reshape(1, c),
        landmark_ids.reshape(1, mine),
        w_msg,
        w_key,
        w_query,
    ]
    to_twin, to_rest, *kept = call_flat(
        functools.partial(send_body, len(given)),
        "send_rows",
        [jax.ShapeDtypeStruct((halo, c), BF16)] * 2
        + [pltpu.VMEM(v.shape, v.dtype) for v in given[1:]],
        [pltpu.with_memory_space_constraint(v, pltpu.HBM) for v in given],
        in_specs=[HBM] * len(given),
        scratch=[
            pltpu.VMEM((1, 2 * halo), jnp.int32),
            pltpu.SemaphoreType.DMA((len(given),)),
        ],
    )
    twin = over_y(to_twin)
    rest = lax.ppermute(
        to_rest, BOTH, [(p, (p + (1 if p % 2 else -1)) % parts) for p in range(parts)]
    )
    (pre,) = call_flat(
        own_body,
        "own_edges",
        [jax.ShapeDtypeStruct((slots, rows, c), F32)],
        kept[:5],
        scratch=[pltpu.VMEM((rows, c), BF16)],
    )
    updated, normed, keys = call_flat(
        edge_body,
        "edges",
        [
            jax.ShapeDtypeStruct((rows, c), BF16),
            jax.ShapeDtypeStruct((rows, c), BF16),
            jax.ShapeDtypeStruct((mine, c), BF16),
        ],
        [*kept[:3], *kept[5:], pre, twin, rest],
        scratch=[pltpu.VMEM((2 * halo, c), BF16)],
    )

    key_blocks = [keys] + [over_z[t](keys) for t in range(1, line)]
    from_x, from_y = over_x(normed), over_y(normed)
    *key_blocks, from_x, from_y = lax.optimization_barrier((*key_blocks, from_x, from_y))
    other_keys = [over_core(jnp.concatenate(key_blocks, axis=0))]
    far = (over_y(from_x[:half]), over_x(from_y[half:]))
    near = (normed, from_x, from_y)
    near_side, side_sums = smooth_up(near, key_blocks, (), "up_near_side")
    *near, side_sums = lax.optimization_barrier((*near, side_sums))
    near_other, other_sums = smooth_up(near, other_keys, (), "up_near_other")
    far_other, other_sums = smooth_up(far, other_keys, (other_sums,), "up_far_other")
    *far, other_sums = lax.optimization_barrier((*far, other_sums))
    far_side, side_sums = smooth_up(far, key_blocks, (side_sums,), "up_far_side")
    core_sums = (side_sums.astype(F32) + over_core(other_sums).astype(F32)).astype(BF16)

    part = mine // 2
    sums = []
    for h in range(2):
        blocks = [core_sums[t * mine + h * part : t * mine + (h + 1) * part] for t in range(line)]
        total = blocks[0].astype(F32)
        for t in range(1, line):
            total = total + over_z[t](blocks[t]).astype(F32)
        total = dot(total.astype(BF16), w_value).astype(BF16)
        side = jnp.concatenate([total] + [over_z[t](total) for t in range(1, line)], axis=0)
        sums.append((side, over_core(side)))

    tiles = [
        tuple(v.reshape(line, mine, v.shape[1]) for v in pair)
        for pair in zip((*near_side, *far_side), (*near_other, *far_other))
    ]
    own_tiles, x_tiles, y_tiles, a_tiles, b_tiles = tiles
    far_jobs = [(a_tiles, 0), (b_tiles, 0)]
    near_jobs = [(x_tiles, 0), (y_tiles, half), (y_tiles, 0), (x_tiles, half)]
    begun = smooth_down([(*j, F32) for j in far_jobs], sums[0], half, "down_far_first", (0,))
    far_a, far_b = smooth_down([(*j, BF16) for j in far_jobs], sums[1], half, "down_far", (1,), begun)
    *both, far_a, far_b = lax.optimization_barrier((*sums[0], *sums[1], far_a, far_b))
    first_a, first_b, pass_a, pass_b = smooth_down(
        [(*j, dtype) for j, dtype in zip(near_jobs, (BF16, BF16, F32, F32))], both, half, "down_near"
    )
    far_a, far_b = over_x(far_a), over_y(far_b)
    first_a, first_b = over_x(first_a), over_y(first_b)
    second_a = over_y((pass_a + far_a.astype(F32)).astype(BF16))
    second_b = over_x((pass_b + far_b.astype(F32)).astype(BF16))
    (own,) = smooth_down([(own_tiles, 0, F32)], both, rows, "down_own")

    return call(
        last_body,
        "last",
        [jax.ShapeDtypeStruct((rows, c), BF16), jax.ShapeDtypeStruct((rows, c), F32)],
        [whole((rows, c))] + [whole((half, c))] * 4 + [whole((rows, c)), whole((c, c))],
        [whole((rows, c))] * 2,
        [own, first_a, second_a, first_b, second_b, updated, w_out],
    )


def solution(mesh):
    split = P(BOTH, None)
    return jax.shard_map(
        functools.partial(shards, mesh.shape["grp"], mesh.shape["dom"]),
        mesh=mesh,
        in_specs=(split, split, P(BOTH), P(BOTH)) + (P(),) * 8,
        out_specs=(split, split),
        check_vma=False,
    )
```

```python
import functools
import math

import jax
import jax.numpy as jnp
from jax import lax
from jax.experimental import pallas as pl
from jax.experimental.pallas import tpu as pltpu
from jax.sharding import PartitionSpec as P

BF16 = jnp.bfloat16
F32 = jnp.float32
BOTH = ("grp", "dom")
EPS = 1e-06
VMEM_LIMIT = 24 * 2**20
LAST_STEPS = 4


def dot(a, b, ca=1, cb=0):
    return lax.dot_general(a, b, (((ca,), (cb,)), ((), ())), preferred_element_type=F32)


VMEM = pl.BlockSpec(memory_space=pltpu.VMEM)
HBM = pl.BlockSpec(memory_space=pltpu.HBM)


def call_flat(body, name, out_shape, args, in_specs=None, out_specs=None, scratch=(), cost=1):
    return pl.pallas_call(
        body,
        in_specs=in_specs or [VMEM] * len(args),
        out_specs=out_specs or [VMEM] * len(out_shape),
        out_shape=out_shape,
        scratch_shapes=list(scratch),
        name=name,
        compiler_params=pltpu.CompilerParams(vmem_limit_bytes=VMEM_LIMIT),
        cost_estimate=pl.CostEstimate(flops=cost, bytes_accessed=1, transcendentals=0),
    )(*args)


def picked(ids, table):
    rows = table.shape[0]
    place = lax.broadcasted_iota(jnp.int32, (rows, ids.shape[1]), 0)
    hot = jnp.where(place == ids, 1.0, 0.0).astype(BF16)
    return dot(hot, table, 0, 0).astype(BF16)


def send_body(count, *refs):
    given, (twin_ref, rest_ref), kept = refs[:count], refs[count : count + 2], refs[count + 2 : -2]
    ids, arrived = refs[-2:]
    copies = [
        pltpu.make_async_copy(src, dst, arrived.at[i])
        for i, (src, dst) in enumerate(zip(given, (ids, *kept)))
    ]
    for copy in copies:
        copy.start()
    copies[0].wait()
    copies[1].wait()
    rows = picked(ids[...], kept[0][...])
    half = rows.shape[0] // 2
    odd = lax.rem(lax.axis_index("dom"), 2) == 1
    twin_ref[...] = jnp.where(odd, rows[:half], rows[half:])
    rest_ref[...] = jnp.where(odd, rows[half:], rows[:half])
    for copy in copies[2:]:
        copy.wait()


def hot_rows(ids, first, width):
    n = ids.shape[1]
    spread = jnp.transpose(jnp.broadcast_to(ids, (128, n)))
    lane = lax.broadcasted_iota(jnp.int32, (n, 128), 1)
    parts = [
        jnp.where(spread == lane + (first + 128 * c), 1.0, 0.0).astype(BF16)
        for c in range(width // 128)
    ]
    return jnp.concatenate(parts, axis=1)


def own_body(nodes, w_src, links, w_dst, bias, pre_ref, source):
    source[...] = dot(nodes[...], w_src[...]).astype(BF16)
    slots, rows = links.shape
    tile = min(rows, 256)
    for first in range(0, rows, tile):
        at = slice(first, first + tile)
        target = dot(nodes[at, :], w_dst[...]) + bias[...]
        for k in range(slots):
            hot = hot_rows(links[k : k + 1, at], 0, rows)
            pre_ref[k, at, :] = dot(hot, source[...]) + target


def twice_gelu(x):
    slope = math.sqrt(2.0 / math.pi)
    return x * (1.0 + jnp.tanh(x * (slope + (0.044715 * slope) * (x * x))))


def edge_body(
    nodes,
    w_src,
    links,
    ids,
    w_msg,
    w_key,
    w_query,
    pre,
    twin,
    rest,
    updated_ref,
    normed_ref,
    keys_ref,
    source,
):
    halo = twin.shape[0]
    slots, rows = links.shape
    odd = lax.rem(lax.axis_index("dom"), 2) == 1
    source[:halo] = dot(jnp.where(odd, twin[...], rest[...]), w_src[...]).astype(BF16)
    source[halo:] = dot(jnp.where(odd, rest[...], twin[...]), w_src[...]).astype(BF16)
    tile = min(rows, 256)
    for first in range(0, rows, tile):
        at = slice(first, first + tile)
        total = 0.0
        for k in range(slots):
            hot = hot_rows(links[k : k + 1, at], rows, 2 * halo)
            total += twice_gelu(pre[k, at, :] + dot(hot, source[...]))
        messages = (total * (0.5 / slots)).astype(BF16)
        updated = (nodes[at, :].astype(F32) + dot(messages, w_msg[...])).astype(BF16)
        updated_ref[at, :] = updated
        wide = updated.astype(F32)
        normed = wide * lax.rsqrt(jnp.mean(wide * wide, axis=1, keepdims=True) + EPS)
        normed_ref[at, :] = normed.astype(BF16)
    keys = dot(picked(ids[...], normed_ref[...]), w_key[...]).astype(BF16)
    keys_ref[...] = dot(keys, w_query[...], 1, 1).astype(BF16)


def smooth_up_body(count, groups, starts, scale, *refs):
    nodes, keys, refs = refs[:count], refs[count : count + groups], refs[count + groups :]
    (sums_ref, held), tiles = refs[-2:], refs[starts:-2]
    first = 0
    for key_ref in keys:
        held[first : first + key_ref.shape[0], :] = key_ref[...]
        first += key_ref.shape[0]
    step = min(first, 512)
    for first in range(0, first, step):
        at = slice(first, first + step)
        total = 0.0
        for start_ref in refs[:starts]:
            total += start_ref[at, :].astype(F32)
        for node_ref, tile_ref in zip(nodes, tiles):
            width = min(node_ref.shape[0], 512)
            for start in range(0, node_ref.shape[0], width):
                block = node_ref[start : start + width, :]
                tile = jnp.exp2(dot(held[at, :], block, 1, 1) * scale).astype(BF16)
                tile_ref[at, start : start + width] = tile
                total += dot(tile, block)
        sums_ref[at, :] = total.astype(BF16)


def smooth_up(blocks, keys, starts, name):
    marks, c = sum(k.shape[0] for k in keys), keys[0].shape[1]
    sizes = [b.shape[0] for b in blocks]
    out = call_flat(
        functools.partial(
            smooth_up_body, len(blocks), len(keys), len(starts), 2.0 * c ** (-0.5) * math.log2(math.e)
        ),
        name,
        [jax.ShapeDtypeStruct((marks, n), BF16) for n in sizes]
        + [jax.ShapeDtypeStruct((marks, c), BF16)],
        [*blocks, *keys, *starts],
        scratch=[pltpu.VMEM((marks, c), BF16)],
        cost=marks * sum(sizes) * c,
    )
    return out[:-1], out[-1]


def smooth_down_body(places, n, given, starts, *refs):
    count = len(places)
    tiles, sums = refs[: 2 * count], refs[2 * count : 2 * count + len(given)]
    begun, outs = refs[2 * count + len(given) : -count], refs[-count:]
    for b, out_ref in enumerate(outs):
        total = begun[b][...] if starts else 0.0
        for place, sum_ref in zip(given, sums):
            tile_ref = tiles[2 * b + place % 2]
            line, mine, _ = tile_ref.shape
            part = mine // 2
            h = place // 2
            tile = tile_ref[:, h * part : (h + 1) * part, places[b] : places[b] + n]
            total += dot(tile.reshape(line * part, n), sum_ref[...], 0, 0)
        out_ref[...] = total.astype(out_ref.dtype)


def smooth_down(jobs, sums, n, name, starts=()):
    given = [i for i, v in enumerate(sums) if v is not None]
    c = sums[given[0]].shape[1]
    return call_flat(
        functools.partial(smooth_down_body, [at for _, at, _ in jobs], n, given, len(starts)),
        name,
        [jax.ShapeDtypeStruct((n, c), dtype) for _, _, dtype in jobs],
        [*(tile for tiles, _, _ in jobs for tile in tiles), *(sums[i] for i in given), *starts],
    )


def last_body(
    own,
    xa,
    ya,
    yb,
    xb,
    updated,
    w_out,
    result_hbm,
    term_hbm,
    result_ref,
    term_ref,
    sent,
):
    rows = own.shape[0]
    step = rows // LAST_STEPS
    copies = []
    for i in range(LAST_STEPS):
        at = slice(i * step, (i + 1) * step)
        first, second = (xa, ya) if 2 * i < LAST_STEPS else (yb, xb)
        there = slice(i * step % (rows // 2), i * step % (rows // 2) + step)
        smooth = own[at, :] + first[there, :].astype(F32) + second[there, :].astype(F32)
        term = smooth * lax.rsqrt(jnp.mean(smooth * smooth, axis=1, keepdims=True) + EPS)
        term_ref[at, :] = term
        copies.append(pltpu.make_async_copy(term_ref.at[at], term_hbm.at[at], sent.at[2 * i]))
        copies[-1].start()
        result = updated[at, :].astype(F32) + dot(term.astype(BF16), w_out[...])
        result_ref[at, :] = result.astype(BF16)
        copies.append(pltpu.make_async_copy(result_ref.at[at], result_hbm.at[at], sent.at[2 * i + 1]))
        copies[-1].start()
    for copy in copies:
        copy.wait()


def shards(
    groups,
    domains,
    nodes,
    neighbours,
    send_rows,
    landmark_ids,
    w_dst,
    w_src,
    w_msg,
    edge_bias,
    w_query,
    w_key,
    w_value,
    w_out,
):
    rows, c = nodes.shape
    halo = send_rows.shape[0] // 2
    mine = landmark_ids.shape[0]
    slots = neighbours.shape[1]
    line = domains // 2
    parts = groups * domains
    half = rows // 2

    def pair(axis, size, flip):
        return lambda v: lax.ppermute(v, axis, [(i, i ^ flip) for i in range(size)])

    over_core = pair("grp", groups, 1)
    over_x = pair("grp", groups, 2)
    over_y = pair("dom", domains, 1)
    over_z = [pair("dom", domains, 2 * t) for t in range(line)]
    given = [
        send_rows.reshape(1, 2 * halo),
        nodes,
        w_src,
        neighbours.T,
        w_dst,
        edge_bias.reshape(1, c),
        landmark_ids.reshape(1, mine),
        w_msg,
        w_key,
        w_query,
    ]
    to_twin, to_rest, *kept = call_flat(
        functools.partial(send_body, len(given)),
        "send_rows",
        [jax.ShapeDtypeStruct((halo, c), BF16)] * 2
        + [pltpu.VMEM(v.shape, v.dtype) for v in given[1:]],
        [pltpu.with_memory_space_constraint(v, pltpu.HBM) for v in given],
        in_specs=[HBM] * len(given),
        scratch=[
            pltpu.VMEM((1, 2 * halo), jnp.int32),
            pltpu.SemaphoreType.DMA((len(given),)),
        ],
    )
    twin = over_y(to_twin)
    rest = lax.ppermute(
        to_rest, BOTH, [(p, (p + (1 if p % 2 else -1)) % parts) for p in range(parts)]
    )
    (pre,) = call_flat(
        own_body,
        "own_edges",
        [jax.ShapeDtypeStruct((slots, rows, c), F32)],
        kept[:5],
        scratch=[pltpu.VMEM((rows, c), BF16)],
    )
    updated, normed, keys = call_flat(
        edge_body,
        "edges",
        [
            jax.ShapeDtypeStruct((rows, c), BF16),
            jax.ShapeDtypeStruct((rows, c), BF16),
            jax.ShapeDtypeStruct((mine, c), BF16),
        ],
        [*kept[:3], *kept[5:], pre, twin, rest],
        scratch=[pltpu.VMEM((2 * halo, c), BF16)],
    )

    key_blocks = [keys] + [over_z[t](keys) for t in range(1, line)]
    from_x, from_y = over_x(normed), over_y(normed)
    *key_blocks, from_x, from_y = lax.optimization_barrier((*key_blocks, from_x, from_y))
    other_keys = [over_core(jnp.concatenate(key_blocks, axis=0))]
    far = (over_y(from_x[:half]), over_x(from_y[half:]))
    near = (normed, from_x, from_y)
    near_side, side_sums = smooth_up(near, key_blocks, (), "up_near_side")
    *near, side_sums = lax.optimization_barrier((*near, side_sums))
    near_other, other_sums = smooth_up(near, other_keys, (), "up_near_other")
    far_other, other_sums = smooth_up(far, other_keys, (other_sums,), "up_far_other")
    *far, other_sums = lax.optimization_barrier((*far, other_sums))
    far_side, side_sums = smooth_up(far, key_blocks, (side_sums,), "up_far_side")
    core_sums = (side_sums.astype(F32) + over_core(other_sums).astype(F32)).astype(BF16)

    part = mine // 2
    sums = []
    for h in range(2):
        blocks = [core_sums[t * mine + h * part : t * mine + (h + 1) * part] for t in range(line)]
        total = blocks[0].astype(F32)
        for t in range(1, line):
            total = total + over_z[t](blocks[t]).astype(F32)
        total = dot(total.astype(BF16), w_value).astype(BF16)
        side = jnp.concatenate([total] + [over_z[t](total) for t in range(1, line)], axis=0)
        sums.append((side, over_core(side)))

    tiles = [
        tuple(v.reshape(line, mine, v.shape[1]) for v in pair)
        for pair in zip((*near_side, *far_side), (*near_other, *far_other))
    ]
    own_tiles, x_tiles, y_tiles, a_tiles, b_tiles = tiles
    far_jobs = [(a_tiles, 0), (b_tiles, 0)]
    near_jobs = [(x_tiles, 0), (y_tiles, half), (y_tiles, 0), (x_tiles, half)]
    begun = smooth_down([(*j, F32) for j in far_jobs], [*sums[0], sums[1][0]], half, "down_far_first")
    far_a, far_b = smooth_down(
        [(*j, BF16) for j in far_jobs], [None, None, None, sums[1][1]], half, "down_far", begun
    )
    *both, far_a, far_b = lax.optimization_barrier((*sums[0], *sums[1], far_a, far_b))
    first_a, first_b, pass_a, pass_b = smooth_down(
        [(*j, dtype) for j, dtype in zip(near_jobs, (BF16, BF16, F32, F32))], both, half, "down_near"
    )
    far_a, far_b = over_x(far_a), over_y(far_b)
    first_a, first_b = over_x(first_a), over_y(first_b)
    second_a = over_y((pass_a + far_a.astype(F32)).astype(BF16))
    second_b = over_x((pass_b + far_b.astype(F32)).astype(BF16))
    (own,) = smooth_down([(own_tiles, 0, F32)], both, rows, "down_own")

    return call_flat(
        last_body,
        "last",
        [pltpu.HBM((rows, c), BF16), pltpu.HBM((rows, c), F32)],
        [own, first_a, second_a, first_b, second_b, updated, w_out],
        out_specs=[HBM] * 2,
        scratch=[
            pltpu.VMEM((rows, c), BF16),
            pltpu.VMEM((rows, c), F32),
            pltpu.SemaphoreType.DMA((2 * LAST_STEPS,)),
        ],
    )


def solution(mesh):
    split = P(BOTH, None)
    return jax.shard_map(
        functools.partial(shards, mesh.shape["grp"], mesh.shape["dom"]),
        mesh=mesh,
        in_specs=(split, split, P(BOTH), P(BOTH)) + (P(),) * 8,
        out_specs=(split, split),
        check_vma=False,
    )
```

```python
import functools
import math

import jax
import jax.numpy as jnp
from jax import lax
from jax.experimental import pallas as pl
from jax.experimental.pallas import tpu as pltpu
from jax.sharding import PartitionSpec as P

BF16 = jnp.bfloat16
F32 = jnp.float32
BOTH = ("grp", "dom")
EPS = 1e-06
VMEM_LIMIT = 24 * 2**20
LAST_STEPS = 2


def dot(a, b, ca=1, cb=0):
    return lax.dot_general(a, b, (((ca,), (cb,)), ((), ())), preferred_element_type=F32)


VMEM = pl.BlockSpec(memory_space=pltpu.VMEM)
HBM = pl.BlockSpec(memory_space=pltpu.HBM)


def call_flat(body, name, out_shape, args, in_specs=None, out_specs=None, scratch=(), cost=1):
    return pl.pallas_call(
        body,
        in_specs=in_specs or [VMEM] * len(args),
        out_specs=out_specs or [VMEM] * len(out_shape),
        out_shape=out_shape,
        scratch_shapes=list(scratch),
        name=name,
        compiler_params=pltpu.CompilerParams(vmem_limit_bytes=VMEM_LIMIT),
        cost_estimate=pl.CostEstimate(flops=cost, bytes_accessed=1, transcendentals=0),
    )(*args)


def picked(ids, table):
    rows = table.shape[0]
    place = lax.broadcasted_iota(jnp.int32, (rows, ids.shape[1]), 0)
    hot = jnp.where(place == ids, 1.0, 0.0).astype(BF16)
    return dot(hot, table, 0, 0).astype(BF16)


def send_body(count, *refs):
    given, (twin_ref, rest_ref), kept = refs[:count], refs[count : count + 2], refs[count + 2 : -2]
    ids, arrived = refs[-2:]
    copies = [
        pltpu.make_async_copy(src, dst, arrived.at[i])
        for i, (src, dst) in enumerate(zip(given, (ids, *kept)))
    ]
    for copy in copies:
        copy.start()
    copies[0].wait()
    copies[1].wait()
    rows = picked(ids[...], kept[0][...])
    half = rows.shape[0] // 2
    odd = lax.rem(lax.axis_index("dom"), 2) == 1
    twin_ref[...] = jnp.where(odd, rows[:half], rows[half:])
    rest_ref[...] = jnp.where(odd, rows[half:], rows[:half])
    for copy in copies[2:]:
        copy.wait()


def hot_rows(ids, first, width):
    n = ids.shape[1]
    spread = jnp.transpose(jnp.broadcast_to(ids, (128, n)))
    lane = lax.broadcasted_iota(jnp.int32, (n, 128), 1)
    parts = [
        jnp.where(spread == lane + (first + 128 * c), 1.0, 0.0).astype(BF16)
        for c in range(width // 128)
    ]
    return jnp.concatenate(parts, axis=1)


def own_body(nodes, w_src, links, w_dst, bias, pre_ref, source):
    source[...] = dot(nodes[...], w_src[...]).astype(BF16)
    slots, rows = links.shape
    tile = min(rows, 256)
    for first in range(0, rows, tile):
        at = slice(first, first + tile)
        target = dot(nodes[at, :], w_dst[...]) + bias[...]
        for k in range(slots):
            hot = hot_rows(links[k : k + 1, at], 0, rows)
            pre_ref[k, at, :] = dot(hot, source[...]) + target


def twice_gelu(x):
    slope = math.sqrt(2.0 / math.pi)
    return x * (1.0 + jnp.tanh(x * (slope + (0.044715 * slope) * (x * x))))


def edge_body(
    nodes,
    w_src,
    links,
    ids,
    w_msg,
    w_key,
    w_query,
    pre,
    twin,
    rest,
    updated_ref,
    normed_ref,
    keys_ref,
    source,
):
    halo = twin.shape[0]
    slots, rows = links.shape
    odd = lax.rem(lax.axis_index("dom"), 2) == 1
    source[:halo] = dot(jnp.where(odd, twin[...], rest[...]), w_src[...]).astype(BF16)
    source[halo:] = dot(jnp.where(odd, rest[...], twin[...]), w_src[...]).astype(BF16)
    tile = min(rows, 256)
    for first in range(0, rows, tile):
        at = slice(first, first + tile)
        total = 0.0
        for k in range(slots):
            hot = hot_rows(links[k : k + 1, at], rows, 2 * halo)
            total += twice_gelu(pre[k, at, :] + dot(hot, source[...]))
        messages = (total * (0.5 / slots)).astype(BF16)
        updated = (nodes[at, :].astype(F32) + dot(messages, w_msg[...])).astype(BF16)
        updated_ref[at, :] = updated
        wide = updated.astype(F32)
        normed = wide * lax.rsqrt(jnp.mean(wide * wide, axis=1, keepdims=True) + EPS)
        normed_ref[at, :] = normed.astype(BF16)
    keys = dot(picked(ids[...], normed_ref[...]), w_key[...]).astype(BF16)
    keys_ref[...] = dot(keys, w_query[...], 1, 1).astype(BF16)


def smooth_up_body(count, groups, starts, scale, *refs):
    nodes, keys, refs = refs[:count], refs[count : count + groups], refs[count + groups :]
    (sums_ref, held), tiles = refs[-2:], refs[starts:-2]
    first = 0
    for key_ref in keys:
        held[first : first + key_ref.shape[0], :] = key_ref[...]
        first += key_ref.shape[0]
    step = min(first, 512)
    for first in range(0, first, step):
        at = slice(first, first + step)
        total = 0.0
        for start_ref in refs[:starts]:
            total += start_ref[at, :].astype(F32)
        for node_ref, tile_ref in zip(nodes, tiles):
            width = min(node_ref.shape[0], 512)
            for start in range(0, node_ref.shape[0], width):
                block = node_ref[start : start + width, :]
                tile = jnp.exp2(dot(held[at, :], block, 1, 1) * scale).astype(BF16)
                tile_ref[at, start : start + width] = tile
                total += dot(tile, block)
        sums_ref[at, :] = total.astype(BF16)


def smooth_up(blocks, keys, starts, name):
    marks, c = sum(k.shape[0] for k in keys), keys[0].shape[1]
    sizes = [b.shape[0] for b in blocks]
    out = call_flat(
        functools.partial(
            smooth_up_body, len(blocks), len(keys), len(starts), 2.0 * c ** (-0.5) * math.log2(math.e)
        ),
        name,
        [jax.ShapeDtypeStruct((marks, n), BF16) for n in sizes]
        + [jax.ShapeDtypeStruct((marks, c), BF16)],
        [*blocks, *keys, *starts],
        scratch=[pltpu.VMEM((marks, c), BF16)],
        cost=marks * sum(sizes) * c,
    )
    return out[:-1], out[-1]


def smooth_down_body(places, n, given, starts, *refs):
    count = len(places)
    tiles, sums = refs[: 2 * count], refs[2 * count : 2 * count + len(given)]
    begun, outs = refs[2 * count + len(given) : -count], refs[-count:]
    for b, out_ref in enumerate(outs):
        total = begun[b][...] if starts else 0.0
        for place, sum_ref in zip(given, sums):
            tile_ref = tiles[2 * b + place % 2]
            line, mine, _ = tile_ref.shape
            part = mine // 2
            h = place // 2
            tile = tile_ref[:, h * part : (h + 1) * part, places[b] : places[b] + n]
            total += dot(tile.reshape(line * part, n), sum_ref[...], 0, 0)
        out_ref[...] = total.astype(out_ref.dtype)


def smooth_down(jobs, sums, n, name, starts=()):
    given = [i for i, v in enumerate(sums) if v is not None]
    c = sums[given[0]].shape[1]
    return call_flat(
        functools.partial(smooth_down_body, [at for _, at, _ in jobs], n, given, len(starts)),
        name,
        [jax.ShapeDtypeStruct((n, c), dtype) for _, _, dtype in jobs],
        [*(tile for tiles, _, _ in jobs for tile in tiles), *(sums[i] for i in given), *starts],
    )


def last_body(
    begun_a,
    begun_b,
    ya,
    xb,
    updated,
    w_out,
    result_hbm,
    term_hbm,
    result_ref,
    term_ref,
    sent,
):
    rows = updated.shape[0]
    step = rows // LAST_STEPS
    copies = []
    for i in range(LAST_STEPS):
        at = slice(i * step, (i + 1) * step)
        begun, second = (begun_a, ya) if 2 * i < LAST_STEPS else (begun_b, xb)
        there = slice(i * step % (rows // 2), i * step % (rows // 2) + step)
        smooth = begun[there, :] + second[there, :].astype(F32)
        term = smooth * lax.rsqrt(jnp.mean(smooth * smooth, axis=1, keepdims=True) + EPS)
        term_ref[at, :] = term
        copies.append(pltpu.make_async_copy(term_ref.at[at], term_hbm.at[at], sent.at[2 * i]))
        copies[-1].start()
        result = updated[at, :].astype(F32) + dot(term.astype(BF16), w_out[...])
        result_ref[at, :] = result.astype(BF16)
        copies.append(pltpu.make_async_copy(result_ref.at[at], result_hbm.at[at], sent.at[2 * i + 1]))
        copies[-1].start()
    for copy in copies:
        copy.wait()


def shards(
    groups,
    domains,
    nodes,
    neighbours,
    send_rows,
    landmark_ids,
    w_dst,
    w_src,
    w_msg,
    edge_bias,
    w_query,
    w_key,
    w_value,
    w_out,
):
    rows, c = nodes.shape
    halo = send_rows.shape[0] // 2
    mine = landmark_ids.shape[0]
    slots = neighbours.shape[1]
    line = domains // 2
    parts = groups * domains
    half = rows // 2

    def pair(axis, size, flip):
        return lambda v: lax.ppermute(v, axis, [(i, i ^ flip) for i in range(size)])

    over_core = pair("grp", groups, 1)
    over_x = pair("grp", groups, 2)
    over_y = pair("dom", domains, 1)
    over_z = [pair("dom", domains, 2 * t) for t in range(line)]
    given = [
        send_rows.reshape(1, 2 * halo),
        nodes,
        w_src,
        neighbours.T,
        w_dst,
        edge_bias.reshape(1, c),
        landmark_ids.reshape(1, mine),
        w_msg,
        w_key,
        w_query,
    ]
    to_twin, to_rest, *kept = call_flat(
        functools.partial(send_body, len(given)),
        "send_rows",
        [jax.ShapeDtypeStruct((halo, c), BF16)] * 2
        + [pltpu.VMEM(v.shape, v.dtype) for v in given[1:]],
        [pltpu.with_memory_space_constraint(v, pltpu.HBM) for v in given],
        in_specs=[HBM] * len(given),
        scratch=[
            pltpu.VMEM((1, 2 * halo), jnp.int32),
            pltpu.SemaphoreType.DMA((len(given),)),
        ],
    )
    twin = over_y(to_twin)
    rest = lax.ppermute(
        to_rest, BOTH, [(p, (p + (1 if p % 2 else -1)) % parts) for p in range(parts)]
    )
    (pre,) = call_flat(
        own_body,
        "own_edges",
        [jax.ShapeDtypeStruct((slots, rows, c), F32)],
        kept[:5],
        scratch=[pltpu.VMEM((rows, c), BF16)],
    )
    updated, normed, keys = call_flat(
        edge_body,
        "edges",
        [
            jax.ShapeDtypeStruct((rows, c), BF16),
            jax.ShapeDtypeStruct((rows, c), BF16),
            jax.ShapeDtypeStruct((mine, c), BF16),
        ],
        [*kept[:3], *kept[5:], pre, twin, rest],
        scratch=[pltpu.VMEM((2 * halo, c), BF16)],
    )

    key_blocks = [keys] + [over_z[t](keys) for t in range(1, line)]
    from_x, from_y = over_x(normed), over_y(normed)
    *key_blocks, from_x, from_y = lax.optimization_barrier((*key_blocks, from_x, from_y))
    other_keys = [over_core(jnp.concatenate(key_blocks, axis=0))]
    far = (over_y(from_x[:half]), over_x(from_y[half:]))
    near = (normed, from_x, from_y)
    near_side, side_sums = smooth_up(near, key_blocks, (), "up_near_side")
    *near, side_sums = lax.optimization_barrier((*near, side_sums))
    near_other, other_sums = smooth_up(near, other_keys, (), "up_near_other")
    far_other, other_sums = smooth_up(far, other_keys, (other_sums,), "up_far_other")
    *far, other_sums = lax.optimization_barrier((*far, other_sums))
    far_side, side_sums = smooth_up(far, key_blocks, (side_sums,), "up_far_side")
    core_sums = (side_sums.astype(F32) + over_core(other_sums).astype(F32)).astype(BF16)

    part = mine // 2
    sums = []
    for h in range(2):
        blocks = [core_sums[t * mine + h * part : t * mine + (h + 1) * part] for t in range(line)]
        total = blocks[0].astype(F32)
        for t in range(1, line):
            total = total + over_z[t](blocks[t]).astype(F32)
        total = dot(total.astype(BF16), w_value).astype(BF16)
        side = jnp.concatenate([total] + [over_z[t](total) for t in range(1, line)], axis=0)
        sums.append((side, over_core(side)))

    tiles = [
        tuple(v.reshape(line, mine, v.shape[1]) for v in pair)
        for pair in zip((*near_side, *far_side), (*near_other, *far_other))
    ]
    own_tiles, x_tiles, y_tiles, a_tiles, b_tiles = tiles
    far_jobs = [(a_tiles, 0), (b_tiles, 0)]
    near_jobs = [(x_tiles, 0), (y_tiles, half), (y_tiles, 0), (x_tiles, half)]
    begun = smooth_down([(*j, F32) for j in far_jobs], [*sums[0], sums[1][0]], half, "down_far_first")
    far_a, far_b = smooth_down(
        [(*j, BF16) for j in far_jobs], [None, None, None, sums[1][1]], half, "down_far", begun
    )
    *both, far_a, far_b = lax.optimization_barrier((*sums[0], *sums[1], far_a, far_b))
    first_a, first_b, pass_a, pass_b = smooth_down(
        [(*j, dtype) for j, dtype in zip(near_jobs, (BF16, BF16, F32, F32))], both, half, "down_near"
    )
    far_a, far_b = over_x(far_a), over_y(far_b)
    first_a, first_b = over_x(first_a), over_y(first_b)
    second_a = over_y((pass_a + far_a.astype(F32)).astype(BF16))
    second_b = over_x((pass_b + far_b.astype(F32)).astype(BF16))
    (own,) = smooth_down([(own_tiles, 0, F32)], both, rows, "down_own")

    begun_a = own[:half] + first_a.astype(F32)
    begun_b = own[half:] + first_b.astype(F32)
    return call_flat(
        last_body,
        "last",
        [pltpu.HBM((rows, c), BF16), pltpu.HBM((rows, c), F32)],
        [begun_a, begun_b, second_a, second_b, updated, w_out],
        out_specs=[HBM] * 2,
        scratch=[
            pltpu.VMEM((rows, c), BF16),
            pltpu.VMEM((rows, c), F32),
            pltpu.SemaphoreType.DMA((2 * LAST_STEPS,)),
        ],
    )


def solution(mesh):
    split = P(BOTH, None)
    return jax.shard_map(
        functools.partial(shards, mesh.shape["grp"], mesh.shape["dom"]),
        mesh=mesh,
        in_specs=(split, split, P(BOTH), P(BOTH)) + (P(),) * 8,
        out_specs=(split, split),
        check_vma=False,
    )
```
